32 devices in a mesh: slab: 2 (over x), pair: 8 (over z, y), quad: 2 (over core).
Axes of the slice: x: 2, y: 2, z: 4, core: 2. Of those that a mesh axis runs over, the one named last changes fastest.
Arguments:
- interferograms: float32 [64, 512, 1024], P(('pair', 'quad'), 'slab'), parts along dimension 1, may hold values from -24 to 24
- pair_epochs: int32 [2, 64], replicated, may hold values from 0 to 31, as said below
- days: int32 [32], replicated, may hold values from 0 to 732, as said below
Outputs:
- smoothed: float32 [32, 512, 1024], P(None, ('slab', 'pair'), 'quad'), parts along dimension 1
The draws below stay inside these ranges and needn't reach their ends.
There are 2 independent parts, one for each index of `slab`. The reference program is written for one: setup_inputs(seed, part) draws one part's arguments, and reference() takes and returns one part's arrays. A program takes and returns all parts, laid end to end along the dimension named above; an argument that names none is the same for every part. Nothing has to cross between parts.
Inputs may be any that keep to these rules, and one draw needn't show every extreme that they name: pair_epochs[0, p] < pair_epochs[1, p] for every pair, the difference is at most 8, and every two consecutive epochs e, e + 1 form one of the pairs. days are strictly increasing, days[0] = 0, consecutive days differ by 12, 24 or 36, and the last day is always the maximum.
All inputs are finite; a program needn't handle non-finite values.
Results may differ from the reference program's by a relative error of at most 0.000071.
Values sent between devices are 32-bit elements; how exact they have to be, the bound alone decides.
A program may use at most 64 MiB of HBM per device.

```python
import jax
import jax.numpy as jnp
from jax import lax

P_SIZE = 64
E = 32
RADIUS = 6
H = 256
W = 1024


def draw_pair_epochs(key, part):
    base = jax.random.fold_in(key, 11)
    key_span, key_start, key_order = jax.random.split(base, 3)
    extra = P_SIZE - (E - 1)
    chain_first = jnp.arange(E - 1).astype(jnp.int32)
    chain_second = chain_first + 1
    spans = jax.random.randint(key_span, (extra,), 2, 9).astype(jnp.int32)
    starts = jax.random.randint(key_start, (extra,), 0, 1 << 20).astype(jnp.int32) % (E - spans)
    first = jnp.concatenate([chain_first, starts])
    second = jnp.concatenate([chain_second, starts + spans])
    order = jax.random.permutation(key_order, P_SIZE)
    return jnp.stack([first[order], second[order]]).astype(jnp.int32)


def draw_days(key, part):
    base = jax.random.fold_in(key, 23)
    shuffled = jax.random.permutation(base, E - 1).astype(jnp.int32)
    gaps = 12 * (1 + shuffled % 3)
    return jnp.concatenate([jnp.zeros((1,), jnp.int32), jnp.cumsum(gaps)]).astype(jnp.int32)


def block_levels(own_key, extent, pieces, smallest, largest):
    gain, own = 1.0, jax.random.fold_in(own_key, 6)
    for axis_at, parts in pieces:
        heights = jnp.exp(jax.random.uniform(jax.random.fold_in(own, axis_at), (parts,), jnp.float32, smallest / len(pieces), largest / len(pieces)))
        gain = gain * jnp.repeat(heights, extent[axis_at] // parts).reshape([-1 if axis == axis_at else 1 for axis in range(len(extent))])
    return gain


def gaussian(rng, dims, scale, bound, cuts=(), kind=jnp.bfloat16):
    loudness = block_levels(rng, dims, cuts, -0.22, 0.18) if cuts else 1.0
    array = jax.random.normal(rng, dims, jnp.float32) * scale * loudness
    return jnp.minimum(jnp.maximum(array, -bound), bound).astype(kind)


def setup_inputs(seed: int = 0, part: int = 0) -> dict:
    streams_of = jax.random.split(jax.random.key(seed), 4)
    part_keys = jax.random.split(jax.random.fold_in(streams_of[3], part), 4)
    interferograms = gaussian(part_keys[0], (P_SIZE, H, W), 3.0, 24.0, ((0, 16),), jnp.float32)
    pair_epochs = draw_pair_epochs(jax.random.fold_in(streams_of[3], 71), part)
    days = draw_days(jax.random.fold_in(streams_of[3], 71), part)
    return {"interferograms": interferograms, "pair_epochs": pair_epochs, "days": days}


def pseudo_inverse(pair_epochs):
    first = pair_epochs[0].astype(jnp.int32)
    second = pair_epochs[1].astype(jnp.int32)
    steps_idx = jnp.arange(E - 1).astype(jnp.int32)
    design = ((first[:, None] <= steps_idx[None, :]) & (steps_idx[None, :] < second[:, None])).astype(jnp.float32)
    normal = jnp.dot(design.T, design, precision=lax.Precision.HIGHEST)
    factor = jnp.linalg.cholesky(normal)
    return jax.scipy.linalg.cho_solve((factor, True), design.T)

def trend_basis(days):
    times = days.astype(jnp.float32)
    scaled = (times - jnp.mean(times)) / 365.25
    phase = 2.0 * jnp.pi * times / 365.25
    basis = jnp.stack([jnp.ones_like(times), scaled, jnp.sin(phase), jnp.cos(phase)], axis=1)
    factor = jnp.linalg.cholesky(jnp.dot(basis.T, basis, precision=lax.Precision.HIGHEST))
    return (basis, factor)

def gauss_taps():
    offsets = (jnp.arange(2 * RADIUS + 1) - RADIUS).astype(jnp.float32)
    weights = jnp.exp(-offsets * offsets / 8.0)
    return weights / jnp.sum(weights)

def reference(interferograms, pair_epochs, days):
    height = interferograms.shape[1]
    width = interferograms.shape[2]
    flat = interferograms.reshape(P_SIZE, height * width)
    pinv = pseudo_inverse(pair_epochs)
    increments = jnp.dot(pinv, flat, precision=lax.Precision.HIGHEST)
    displacement = jnp.concatenate([jnp.zeros((1, height * width), jnp.float32), jnp.cumsum(increments, axis=0)], axis=0)
    basis, factor = trend_basis(days)
    coefficients = jax.scipy.linalg.cho_solve((factor, True), jnp.dot(basis.T, displacement, precision=lax.Precision.HIGHEST))
    detrended = displacement - jnp.dot(basis, coefficients, precision=lax.Precision.HIGHEST)
    detrended = detrended.reshape(E, height, width)
    taps = gauss_taps()
    padded = jnp.pad(detrended, ((0, 0), (0, 0), (RADIUS, RADIUS)))
    across = taps[0] * padded[:, :, 0:width]
    for shift in range(1, 2 * RADIUS + 1):
        across = across + taps[shift] * padded[:, :, shift:shift + width]
    padded = jnp.pad(across, ((0, 0), (RADIUS, RADIUS), (0, 0)))
    smoothed = taps[0] * padded[:, 0:height, :]
    for shift in range(1, 2 * RADIUS + 1):
        smoothed = smoothed + taps[shift] * padded[:, shift:shift + height, :]
    return smoothed
```

```python
import functools
import math

import jax
import jax.numpy as jnp
from jax import lax
from jax.experimental import pallas as pl
from jax.experimental.pallas import tpu as pltpu
from jax.sharding import PartitionSpec as P

E = 32
RADIUS = 6
STRIP = 8
LANES = 128
MESH = pl.DeviceIdType.MESH
HIGHEST = lax.Precision.HIGHEST


def gauss_taps():
    weights = [math.exp(-i * i / 8.0) for i in range(-RADIUS, RADIUS + 1)]
    return [w / sum(weights) for w in weights]


def iota(shape, dim):
    return lax.broadcasted_iota(jnp.int32, shape, dim)


def smooth_strip(block):
    taps = gauss_taps()
    tall, width = block.shape
    mid = slice(STRIP, 2 * STRIP)
    total = taps[RADIUS] * block[mid]
    for i in range(1, RADIUS + 1):
        pair = pltpu.roll(block, i, 0)[mid] + pltpu.roll(block, tall - i, 0)[mid]
        total = total + taps[RADIUS + i] * pair
    wide = jnp.concatenate([total, jnp.zeros((STRIP, LANES), jnp.float32)], axis=1)
    span = width + LANES
    total = taps[RADIUS] * wide
    for i in range(1, RADIUS + 1):
        pair = pltpu.roll(wide, i, 1) + pltpu.roll(wide, span - i, 1)
        total = total + taps[RADIUS + i] * pair
    return total[:, :width]


def epoch_weights(pair_epochs, days):
    pairs = pair_epochs.shape[1]
    first, second = pair_epochs[0:1], pair_epochs[1:2]
    step = iota((E, pairs), 0)
    design_t = jnp.where((first <= step) & (step < second), 1.0, 0.0)
    row, col = iota((LANES, pairs), 0), iota((LANES, pairs), 1)
    inside = (row < E) & (first <= row) & (row < second)
    other = jnp.where(inside | (row == col + E), 1.0, 0.0)
    system = lax.dot_general(
        design_t, other, (((1,), (1,)), ((), ())), precision=HIGHEST, preferred_element_type=jnp.float32
    )
    row, col = iota((E, LANES), 0), iota((E, LANES), 1)
    system = system + jnp.where((row == E - 1) & (col == E - 1), 1.0, 0.0)

    def eliminate(k, a):
        pivot_row = jnp.sum(jnp.where(row == k, a, 0.0), axis=0, keepdims=True)
        pivot_col = jnp.sum(jnp.where(col == k, a, 0.0), axis=1, keepdims=True)
        pivot = jnp.sum(jnp.where(col[0:1] == k, pivot_row, 0.0), axis=1, keepdims=True)
        scaled = pivot_row / pivot
        return jnp.where(row == k, scaled, a - pivot_col * scaled)

    system = lax.fori_loop(0, E, eliminate, system)

    times = days.astype(jnp.float32)
    centred = (times - jnp.sum(times, axis=1, keepdims=True) / E) / 365.25
    phase = 2.0 * math.pi * times / 365.25
    erow, ecol = iota((E, E), 0), iota((E, E), 1)
    rest = jnp.where(erow == ecol, 1.0, 0.0)
    basis = []
    for column in (jnp.ones_like(times), centred, jnp.sin(phase), jnp.cos(phase)):
        for _ in range(2):
            for q in basis:
                column = column - q * jnp.sum(q * column, axis=1, keepdims=True)
        column = column / jnp.sqrt(jnp.sum(column * column, axis=1, keepdims=True))
        basis.append(column)
        upright = jnp.sum(jnp.where(erow == ecol, column, 0.0), axis=1, keepdims=True)
        rest = rest - upright * column
    summing = jnp.where(ecol < erow, 1.0, 0.0)
    displacement = jnp.dot(summing, system, precision=HIGHEST, preferred_element_type=jnp.float32)
    return jnp.dot(rest, displacement, precision=HIGHEST, preferred_element_type=jnp.float32)


def spread_weights(weights, pairs):
    tall, wide = E * STRIP, pairs * STRIP
    right = jnp.where(iota((LANES, wide), 0) == iota((LANES, wide), 1) // STRIP + E, 1.0, 0.0)
    left = jnp.where(iota((tall, E), 1) == iota((tall, E), 0) // STRIP, 1.0, 0.0)
    full = jnp.dot(weights, right, precision=HIGHEST, preferred_element_type=jnp.float32)
    full = jnp.dot(left, full, precision=HIGHEST, preferred_element_type=jnp.float32)
    same = iota((tall, wide), 0) % STRIP == iota((tall, wide), 1) % STRIP
    return jnp.where(same, full, 0.0)


def kernel(n_pair, n_quad, x_hbm, epochs_ref, days_ref, out_hbm, padded, ready, held, spread, result, in_sem, send_sem, recv_sem, out_sem):
    local, height, width = ready.shape
    n = n_pair * n_quad
    rows, cols = height // n_pair, width // n_quad
    strips = rows // STRIP
    slab = lax.axis_index("slab")
    my_pair = lax.axis_index("pair")
    my_quad = lax.axis_index("quad")
    me = my_pair * n_quad + my_quad

    loads = [
        pltpu.make_async_copy(x_hbm.at[l], padded.at[l, pl.ds(STRIP, height), :], in_sem.at[l]) for l in range(local)
    ]
    for load in loads:
        load.start()
    barrier = pltpu.get_barrier_semaphore()

    def greet(j, carry):
        other = lax.rem(me + j, n)
        pl.semaphore_signal(
            barrier, inc=1, device_id=(slab, other // n_quad, other % n_quad), device_id_type=MESH
        )
        return carry

    lax.fori_loop(1, n, greet, 0)
    edge = jnp.zeros((local, STRIP, width), jnp.float32)
    padded[:, 0:STRIP, :] = edge
    padded[:, STRIP + height : 2 * STRIP + height, :] = edge
    for load in loads:
        load.wait()
    pl.semaphore_wait(barrier, n - 1)

    def part(t, pair, quad):
        at_row = pl.multiple_of(pair * rows + t * STRIP, STRIP)
        at_col = pl.multiple_of(quad * cols, LANES)
        return ready.at[:, pl.ds(at_row, STRIP), pl.ds(at_col, cols)]

    def slot(t, source):
        return held.at[source, :, pl.ds(pl.multiple_of(t * STRIP, STRIP), STRIP), :]

    def send(t, pair, quad):
        return pltpu.make_async_remote_copy(
            src_ref=part(t, pair, quad),
            dst_ref=slot(t, me),
            send_sem=send_sem.at[t, pair * n_quad + quad],
            recv_sem=recv_sem.at[t, me],
            device_id=(slab, pair, quad),
            device_id_type=MESH,
        )

    def produce(i, carry):
        t, s = i // n_pair, i % n_pair
        away = n_pair // 2 + (1 - 2 * (s % 2)) * ((s + 1) // 2)
        pair = (my_pair + away + n_pair) % n_pair
        at_row = pl.multiple_of(pair * rows + t * STRIP, STRIP)
        for l in range(local):
            ready[l, pl.ds(at_row, STRIP), :] = smooth_strip(padded[l, pl.ds(at_row, 3 * STRIP), :])
        for j in range(1, n_quad):
            send(t, pair, (my_quad + j) % n_quad).start()

        @pl.when(pair != my_pair)
        def _():
            send(t, pair, my_quad).start()

        @pl.when(pair == my_pair)
        def _():
            pltpu.make_async_copy(part(t, my_pair, my_quad), slot(t, me), recv_sem.at[t, me]).start()

        return carry

    lax.fori_loop(0, strips * n_pair, produce, 0)

    spread[...] = spread_weights(epoch_weights(epochs_ref[...], days_ref[...]), local * n)

    def out_copy(t):
        at = pl.ds(pl.multiple_of(t * STRIP, STRIP), STRIP)
        return pltpu.make_async_copy(result.at[:, at, :], out_hbm.at[:, at, :], out_sem.at[t])

    def consume(t, carry):
        def arrived(source, carry):
            pltpu.make_async_copy(slot(t, source), slot(t, source), recv_sem.at[t, source]).wait()
            return carry

        lax.fori_loop(0, n, arrived, 0)
        at = pl.ds(pl.multiple_of(t * STRIP, STRIP), STRIP)
        stack = held[:, :, at, :].reshape(n * local * STRIP, cols)
        total = jnp.dot(spread[...], stack, precision=HIGHEST, preferred_element_type=jnp.float32)
        result[:, at, :] = total.reshape(E, STRIP, cols)
        out_copy(t).start()
        return carry

    lax.fori_loop(0, strips, consume, 0)

    def sent(i, carry):
        t, other = i // (n - 1), lax.rem(me + 1 + i % (n - 1), n)
        send(t, other // n_quad, other % n_quad).wait_send()
        return carry

    lax.fori_loop(0, strips * (n - 1), sent, 0)
    for t in range(strips):
        out_copy(t).wait()


def shards(interferograms, pair_epochs, days):
    n_pair = lax.axis_size("pair")
    n_quad = lax.axis_size("quad")
    n = n_pair * n_quad
    local, height, width = interferograms.shape
    rows, cols = height // n_pair, width // n_quad
    strips = rows // STRIP
    pairs = local * n
    return pl.pallas_call(
        functools.partial(kernel, n_pair, n_quad),
        out_shape=jax.ShapeDtypeStruct((E, rows, cols), jnp.float32),
        in_specs=[
            pl.BlockSpec(memory_space=pl.ANY),
            pl.BlockSpec(memory_space=pltpu.VMEM),
            pl.BlockSpec(memory_space=pltpu.VMEM),
        ],
        out_specs=pl.BlockSpec(memory_space=pl.ANY),
        scratch_shapes=[
            pltpu.VMEM((local, height + 2 * STRIP, width), jnp.float32),
            pltpu.VMEM((local, height, width), jnp.float32),
            pltpu.VMEM((n, local, rows, cols), jnp.float32),
            pltpu.VMEM((E * STRIP, pairs * STRIP), jnp.float32),
            pltpu.VMEM((E, rows, cols), jnp.float32),
            pltpu.SemaphoreType.DMA((local,)),
            pltpu.SemaphoreType.DMA((strips, n)),
            pltpu.SemaphoreType.DMA((strips, n)),
            pltpu.SemaphoreType.DMA((strips,)),
        ],
        compiler_params=pltpu.CompilerParams(
            collective_id=0, has_side_effects=True, vmem_limit_bytes=48 * 1024 * 1024
        ),
        name="smooth_and_invert",
    )(interferograms, pair_epochs, days[None, :])


def solution(mesh):
    placed = (P(("pair", "quad"), "slab", None), P(), P())
    return jax.shard_map(
        shards,
        mesh=mesh,
        in_specs=placed,
        out_specs=P(None, ("slab", "pair"), "quad"),
        check_vma=False,
    )
```

```python
import functools
import math

import jax
import jax.numpy as jnp
from jax import lax
from jax.experimental import pallas as pl
from jax.experimental.pallas import tpu as pltpu
from jax.sharding import PartitionSpec as P

E = 32
RADIUS = 6
STRIP = 8
LANES = 128
MESH = pl.DeviceIdType.MESH
HIGHEST = lax.Precision.HIGHEST


def gauss_taps():
    weights = [math.exp(-i * i / 8.0) for i in range(-RADIUS, RADIUS + 1)]
    return [w / sum(weights) for w in weights]


def iota(shape, dim):
    return lax.broadcasted_iota(jnp.int32, shape, dim)


def smooth_rows(column, at_row):
    taps = gauss_taps()
    rows = [column[pl.ds(at_row + STRIP - RADIUS + i, STRIP), :] for i in range(2 * RADIUS + 1)]
    total = taps[RADIUS] * rows[RADIUS]
    for i in range(1, RADIUS + 1):
        total = total + taps[RADIUS + i] * (rows[RADIUS - i] + rows[RADIUS + i])
    return total


def smooth_columns(columns):
    taps = gauss_taps()
    wide = jnp.concatenate(columns + [jnp.zeros_like(columns[0])], axis=1)
    span = wide.shape[1]
    total = taps[RADIUS] * wide
    for i in range(1, RADIUS + 1):
        total = total + taps[RADIUS + i] * (pltpu.roll(wide, i, 1) + pltpu.roll(wide, span - i, 1))
    return total[:, : span - LANES]


def pick(step, table):
    return sum(jnp.where(step == k, value, 0) for k, value in enumerate(table))


def visits(n_outer, n_inner):
    far = sorted(range(n_outer), key=lambda d: -min(d, n_outer - d))
    straight = [(d, 0) for d in far if d]
    bent = [(d, i) for i in range(1, n_inner) for d in reversed(far)]
    order = []
    while straight or bent:
        order += straight[:1] + bent[:1]
        straight, bent = straight[1:], bent[1:]
    return order + [(0, 0)]


def epoch_weights(pair_epochs, days):
    pairs = pair_epochs.shape[1]
    first, second = pair_epochs[0:1], pair_epochs[1:2]
    step = iota((E, pairs), 0)
    design_t = jnp.where((first <= step) & (step < second), 1.0, 0.0)
    row, col = iota((LANES, pairs), 0), iota((LANES, pairs), 1)
    inside = (row < E) & (first <= row) & (row < second)
    other = jnp.where(inside | (row == col + E), 1.0, 0.0)
    system = lax.dot_general(
        design_t, other, (((1,), (1,)), ((), ())), precision=HIGHEST, preferred_element_type=jnp.float32
    )
    row, col = iota((E, LANES), 0), iota((E, LANES), 1)
    system = system + jnp.where((row == E - 1) & (col == E - 1), 1.0, 0.0)

    def eliminate(k, a):
        pivot_row = jnp.sum(jnp.where(row == k, a, 0.0), axis=0, keepdims=True)
        pivot_col = jnp.sum(jnp.where(col == k, a, 0.0), axis=1, keepdims=True)
        pivot = jnp.sum(jnp.where(col[0:1] == k, pivot_row, 0.0), axis=1, keepdims=True)
        scaled = pivot_row / pivot
        return jnp.where(row == k, scaled, a - pivot_col * scaled)

    system = lax.fori_loop(0, E, eliminate, system)

    times = days.astype(jnp.float32)
    centred = (times - jnp.sum(times, axis=1, keepdims=True) / E) / 365.25
    phase = 2.0 * math.pi * times / 365.25
    erow, ecol = iota((E, E), 0), iota((E, E), 1)
    rest = jnp.where(erow == ecol, 1.0, 0.0)
    basis = []
    for column in (jnp.ones_like(times), centred, jnp.sin(phase), jnp.cos(phase)):
        for _ in range(2):
            for q in basis:
                column = column - q * jnp.sum(q * column, axis=1, keepdims=True)
        column = column / jnp.sqrt(jnp.sum(column * column, axis=1, keepdims=True))
        basis.append(column)
        upright = jnp.sum(jnp.where(erow == ecol, column, 0.0), axis=1, keepdims=True)
        rest = rest - upright * column
    summing = jnp.where(ecol < erow, 1.0, 0.0)
    displacement = jnp.dot(summing, system, precision=HIGHEST, preferred_element_type=jnp.float32)
    return jnp.dot(rest, displacement, precision=HIGHEST, preferred_element_type=jnp.float32)


def spread_weights(weights, pairs):
    tall, wide = E * STRIP, pairs * STRIP
    right = jnp.where(iota((LANES, wide), 0) == iota((LANES, wide), 1) // STRIP + E, 1.0, 0.0)
    left = jnp.where(iota((tall, E), 1) == iota((tall, E), 0) // STRIP, 1.0, 0.0)
    full = jnp.dot(weights, right, precision=HIGHEST, preferred_element_type=jnp.float32)
    full = jnp.dot(left, full, precision=HIGHEST, preferred_element_type=jnp.float32)
    same = iota((tall, wide), 0) % STRIP == iota((tall, wide), 1) % STRIP
    return jnp.where(same, full, 0.0)


def kernel(n_pair, n_quad, n_inner, x_hbm, epochs_hbm, days_hbm, out_hbm, padded, ready, held, spread, result, epochs_ref, days_ref, in_sem, small_sem, send_sem, recv_sem, out_sem):
    local, height, width = ready.shape
    n = n_pair * n_quad
    rows, cols = height // n_pair, width // n_quad
    strips = rows // STRIP
    slab = lax.axis_index("slab")
    my_pair = lax.axis_index("pair")
    my_quad = lax.axis_index("quad")
    me = my_pair * n_quad + my_quad

    tiles = width // LANES
    loads = [
        pltpu.make_async_copy(
            x_hbm.at[l, :, pl.ds(j * LANES, LANES)],
            padded.at[l, j, pl.ds(STRIP, height), :],
            in_sem.at[l, j],
        )
        for l in range(local)
        for j in range(tiles)
    ]
    loads += [
        pltpu.make_async_copy(epochs_hbm, epochs_ref, small_sem.at[0]),
        pltpu.make_async_copy(days_hbm, days_ref, small_sem.at[1]),
    ]
    for load in loads:
        load.start()
    barrier = pltpu.get_barrier_semaphore()

    def greet(j, carry):
        other = lax.rem(me + j, n)
        pl.semaphore_signal(
            barrier, inc=1, device_id=(slab, other // n_quad, other % n_quad), device_id_type=MESH
        )
        return carry

    lax.fori_loop(1, n, greet, 0)
    edge = jnp.zeros((local, tiles, STRIP, LANES), jnp.float32)
    padded[:, :, 0:STRIP, :] = edge
    padded[:, :, STRIP + height : 2 * STRIP + height, :] = edge
    for load in loads:
        load.wait()
    pl.semaphore_wait(barrier, n - 1)

    def part(t, pair, quad):
        at_row = pl.multiple_of(pair * rows + t * STRIP, STRIP)
        at_col = pl.multiple_of(quad * cols, LANES)
        return ready.at[:, pl.ds(at_row, STRIP), pl.ds(at_col, cols)]

    def slot(t, source):
        return held.at[source, :, pl.ds(pl.multiple_of(t * STRIP, STRIP), STRIP), :]

    def send(t, pair, quad):
        return pltpu.make_async_remote_copy(
            src_ref=part(t, pair, quad),
            dst_ref=slot(t, me),
            send_sem=send_sem.at[t, pair * n_quad + quad],
            recv_sem=recv_sem.at[t, me],
            device_id=(slab, pair, quad),
            device_id_type=MESH,
        )

    n_outer = n_pair // n_inner
    order = visits(n_outer, n_inner)

    def produce(i, carry):
        t, s = i // n_pair, i % n_pair
        outer = (my_pair // n_inner + pick(s, [o for o, _ in order])) % n_outer
        inner = (my_pair % n_inner + pick(s, [i for _, i in order])) % n_inner
        pair = outer * n_inner + inner
        at_row = pl.multiple_of(pair * rows + t * STRIP, STRIP)
        for l in range(local):
            columns = [smooth_rows(padded.at[l, j], at_row) for j in range(tiles)]
            ready[l, pl.ds(at_row, STRIP), :] = smooth_columns(columns)
        for j in range(1, n_quad):
            send(t, pair, (my_quad + j) % n_quad).start()

        @pl.when(pair != my_pair)
        def _():
            send(t, pair, my_quad).start()

        @pl.when(pair == my_pair)
        def _():
            pltpu.make_async_copy(part(t, my_pair, my_quad), slot(t, me), recv_sem.at[t, me]).start()

        return carry

    lax.fori_loop(0, strips * n_pair, produce, 0)

    spread[...] = spread_weights(epoch_weights(epochs_ref[...], days_ref[...]), local * n)

    def out_copy(t):
        at = pl.ds(pl.multiple_of(t * STRIP, STRIP), STRIP)
        return pltpu.make_async_copy(result.at[:, at, :], out_hbm.at[:, at, :], out_sem.at[t])

    def consume(t, carry):
        def arrived(source, carry):
            pltpu.make_async_copy(slot(t, source), slot(t, source), recv_sem.at[t, source]).wait()
            return carry

        lax.fori_loop(0, n, arrived, 0)
        at = pl.ds(pl.multiple_of(t * STRIP, STRIP), STRIP)
        stack = held[:, :, at, :].reshape(n * local * STRIP, cols)
        total = jnp.dot(spread[...], stack, precision=HIGHEST, preferred_element_type=jnp.float32)
        result[:, at, :] = total.reshape(E, STRIP, cols)
        out_copy(t).start()
        return carry

    lax.fori_loop(0, strips, consume, 0)

    def sent(i, carry):
        t, other = i // (n - 1), lax.rem(me + 1 + i % (n - 1), n)
        send(t, other // n_quad, other % n_quad).wait_send()
        return carry

    lax.fori_loop(0, strips * (n - 1), sent, 0)
    for t in range(strips):
        out_copy(t).wait()


def shards(n_inner, interferograms, pair_epochs, days):
    n_pair = lax.axis_size("pair")
    n_quad = lax.axis_size("quad")
    n = n_pair * n_quad
    local, height, width = interferograms.shape
    rows, cols = height // n_pair, width // n_quad
    strips = rows // STRIP
    pairs = local * n
    return pl.pallas_call(
        functools.partial(kernel, n_pair, n_quad, n_inner),
        out_shape=jax.ShapeDtypeStruct((E, rows, cols), jnp.float32),
        in_specs=[pl.BlockSpec(memory_space=pl.ANY)] * 3,
        out_specs=pl.BlockSpec(memory_space=pl.ANY),
        scratch_shapes=[
            pltpu.VMEM((local, width // LANES, height + 2 * STRIP, LANES), jnp.float32),
            pltpu.VMEM((local, height, width), jnp.float32),
            pltpu.VMEM((n, local, rows, cols), jnp.float32),
            pltpu.VMEM((E * STRIP, pairs * STRIP), jnp.float32),
            pltpu.VMEM((E, rows, cols), jnp.float32),
            pltpu.VMEM(pair_epochs.shape, jnp.int32),
            pltpu.VMEM((1,) + days.shape, jnp.int32),
            pltpu.SemaphoreType.DMA((local, width // LANES)),
            pltpu.SemaphoreType.DMA((2,)),
            pltpu.SemaphoreType.DMA((strips, n)),
            pltpu.SemaphoreType.DMA((strips, n)),
            pltpu.SemaphoreType.DMA((strips,)),
        ],
        compiler_params=pltpu.CompilerParams(
            collective_id=0, has_side_effects=True, vmem_limit_bytes=48 * 1024 * 1024
        ),
        name="smooth_and_invert",
    )(interferograms, pair_epochs, days[None, :])


def inner_size(mesh):
    line = list(mesh.devices[0, :, 0])
    coords = [getattr(d, "coords", None) for d in line]
    if any(c is None for c in coords):
        return 1
    moving = [k for k in range(len(coords[0])) if coords[0][k] != coords[-1][k]]
    for k in moving:
        run = 1
        while run < len(line) and coords[run][k] == coords[0][k]:
            run += 1
        if 1 < run < len(line) and len(line) % run == 0:
            return run
    return 1


def solution(mesh):
    placed = (P(("pair", "quad"), "slab", None), P(), P())
    return jax.shard_map(
        functools.partial(shards, inner_size(mesh)),
        mesh=mesh,
        in_specs=placed,
        out_specs=P(None, ("slab", "pair"), "quad"),
        check_vma=False,
    )
```

```python
import functools
import math

import jax
import jax.numpy as jnp
from jax import lax
from jax.experimental import pallas as pl
from jax.experimental.pallas import tpu as pltpu
from jax.sharding import PartitionSpec as P

E = 32
RADIUS = 6
STRIP = 8
LANES = 128
MESH = pl.DeviceIdType.MESH
HIGHEST = lax.Precision.HIGHEST
TERMS = 4


def gauss_taps():
    weights = [math.exp(-i * i / 8.0) for i in range(-RADIUS, RADIUS + 1)]
    return [w / sum(weights) for w in weights]


def iota(shape, dim):
    return lax.broadcasted_iota(jnp.int32, shape, dim)


def smooth_rows(column, at_row):
    taps = gauss_taps()
    rows = [column[pl.ds(at_row + STRIP - RADIUS + i, STRIP), :] for i in range(2 * RADIUS + 1)]
    total = taps[RADIUS] * rows[RADIUS]
    for i in range(1, RADIUS + 1):
        total = total + taps[RADIUS + i] * (rows[RADIUS - i] + rows[RADIUS + i])
    return total


def smooth_columns(columns):
    taps = gauss_taps()
    wide = jnp.concatenate(columns + [jnp.zeros_like(columns[0])], axis=1)
    span = wide.shape[1]
    total = taps[RADIUS] * wide
    for i in range(1, RADIUS + 1):
        total = total + taps[RADIUS + i] * (pltpu.roll(wide, i, 1) + pltpu.roll(wide, span - i, 1))
    return total[:, : span - LANES]


def pair_weights(pair_epochs, days):
    pairs = pair_epochs.shape[1]
    first, second = pair_epochs[0:1], pair_epochs[1:2]
    step = iota((E, pairs), 0)
    design_t = jnp.where((first <= step) & (step < second), 1.0, 0.0)
    row, col = iota((LANES, pairs), 0), iota((LANES, pairs), 1)
    inside = (row < E) & (first <= row) & (row < second)
    other = jnp.where(inside | (row == col + E), 1.0, 0.0)
    system = lax.dot_general(
        design_t, other, (((1,), (1,)), ((), ())), precision=HIGHEST, preferred_element_type=jnp.float32
    )
    row, col = iota((E, LANES), 0), iota((E, LANES), 1)
    system = system + jnp.where((row == E - 1) & (col == E - 1), 1.0, 0.0)

    def eliminate(k, a):
        pivot_row = jnp.sum(jnp.where(row == k, a, 0.0), axis=0, keepdims=True)
        pivot_col = jnp.sum(jnp.where(col == k, a, 0.0), axis=1, keepdims=True)
        pivot = jnp.sum(jnp.where(col[0:1] == k, pivot_row, 0.0), axis=1, keepdims=True)
        scaled = pivot_row / pivot
        return jnp.where(row == k, scaled, a - pivot_col * scaled)

    system = lax.fori_loop(0, E, eliminate, system)

    times = days.astype(jnp.float32)
    centred = (times - jnp.sum(times, axis=1, keepdims=True) / E) / 365.25
    phase = 2.0 * math.pi * times / 365.25
    erow, ecol = iota((E, E), 0), iota((E, E), 1)
    lane = ecol[0:1]
    eye = jnp.where(erow == ecol, 1.0, 0.0)
    q, q_t = eye, eye
    columns = [jnp.ones_like(times), centred, jnp.sin(phase), jnp.cos(phase)]
    for j in range(TERMS):
        below = jnp.where(lane >= j, columns[j], 0.0)
        head = jnp.sum(jnp.where(lane == j, below, 0.0), axis=1, keepdims=True)
        norm = jnp.sqrt(jnp.sum(below * below, axis=1, keepdims=True))
        v = below + jnp.where(lane == j, jnp.where(head >= 0, norm, -norm), 0.0)
        v = v * lax.rsqrt(0.5 * jnp.sum(v * v, axis=1, keepdims=True))
        upright = jnp.sum(jnp.where(erow == ecol, v, 0.0), axis=1, keepdims=True)
        columns = [c - v * jnp.sum(v * c, axis=1, keepdims=True) for c in columns]
        q = q - jnp.sum(q * v, axis=1, keepdims=True) * v
        q_t = q_t - upright * jnp.sum(q_t * upright, axis=0, keepdims=True)
    q = jnp.where(ecol >= TERMS, q, 0.0)
    q_t = jnp.where(erow >= TERMS, q_t, 0.0)
    summing = jnp.where(ecol < erow, 1.0, 0.0)
    displacement = jnp.dot(summing, system, precision=HIGHEST, preferred_element_type=jnp.float32)
    return q, jnp.dot(q_t, displacement, precision=HIGHEST, preferred_element_type=jnp.float32)


def spread_weights(weights, first, count):
    tall, wide, depth = E * STRIP, count * STRIP, weights.shape[1]
    right = jnp.where(iota((depth, wide), 0) == iota((depth, wide), 1) // STRIP + first, 1.0, 0.0)
    left = jnp.where(iota((tall, E), 1) == iota((tall, E), 0) // STRIP, 1.0, 0.0)
    full = jnp.dot(weights, right, precision=HIGHEST, preferred_element_type=jnp.float32)
    full = jnp.dot(left, full, precision=HIGHEST, preferred_element_type=jnp.float32)
    same = iota((tall, wide), 0) % STRIP == iota((tall, wide), 1) % STRIP
    return jnp.where(same, full, 0.0)


def times_stack(weights, stack):
    flat = stack.reshape(weights.shape[1], stack.shape[-1])
    total = jnp.dot(weights, flat, precision=HIGHEST, preferred_element_type=jnp.float32)
    return total.reshape(E, STRIP, stack.shape[-1])


def raw_strips(n_outer, strips):
    return 1 if n_outer > 1 and n_outer // 2 <= 2 else strips


def kernel(
    n_pair, n_quad, n_inner,
    x_hbm, epochs_hbm, days_hbm, out_hbm,
    padded, ready, held, gathered, summed, arrived, spread, result, epochs_ref, days_ref,
    in_sem, small_sem, send_sem, recv_sem, gather_sem, sum_send_sem, sum_recv_sem, out_sem,
):
    local, height, width = ready.shape
    n = n_pair * n_quad
    n_outer = n_pair // n_inner
    half_n, half_pair = n // 2, n_pair // 2
    far = n_outer // 2
    rows, cols = height // n_pair, width // n_quad
    strips = rows // STRIP
    raw = raw_strips(n_outer, strips)
    tiles = width // LANES
    slab = lax.axis_index("slab")
    my_pair = lax.axis_index("pair")
    my_quad = lax.axis_index("quad")
    me = my_pair * n_quad + my_quad
    side = my_pair // half_pair
    my_source = me % half_n
    my_inner = my_pair % n_inner
    edge_outer = far - 1 + side

    loads = [
        pltpu.make_async_copy(
            x_hbm.at[l, :, pl.ds(j * LANES, LANES)],
            padded.at[l, j, pl.ds(STRIP, height), :],
            in_sem.at[l, j],
        )
        for l in range(local)
        for j in range(tiles)
    ]
    loads += [
        pltpu.make_async_copy(epochs_hbm, epochs_ref, small_sem.at[0]),
        pltpu.make_async_copy(days_hbm, days_ref, small_sem.at[1]),
    ]
    for load in loads:
        load.start()
    barrier = pltpu.get_barrier_semaphore()

    def greet(j, carry):
        other = lax.rem(me + j, n)
        pl.semaphore_signal(
            barrier, inc=1, device_id=(slab, other // n_quad, other % n_quad), device_id_type=MESH
        )
        return carry

    lax.fori_loop(1, n, greet, 0)
    edge = jnp.zeros((local, tiles, STRIP, LANES), jnp.float32)
    padded[:, :, 0:STRIP, :] = edge
    padded[:, :, STRIP + height : 2 * STRIP + height, :] = edge
    if raw < strips:
        arrived[0:TERMS] = jnp.zeros((TERMS, rows, cols), jnp.float32)
    for load in loads:
        load.wait()
    pl.semaphore_wait(barrier, n - 1)

    def strip_rows(t):
        return pl.ds(pl.multiple_of(t * STRIP, STRIP), STRIP)

    def part(t, pair, quad):
        at_row = pl.multiple_of(pair * rows + t * STRIP, STRIP)
        at_col = pl.multiple_of(quad * cols, LANES)
        return ready.at[:, pl.ds(at_row, STRIP), pl.ds(at_col, cols)]

    def slot(t, source):
        return held.at[source, :, strip_rows(t), :]

    def gather_slot(t, at, source):
        return gathered.at[at, source, :, strip_rows(t), :]

    def send(t, pair, quad):
        return pltpu.make_async_remote_copy(
            src_ref=part(t, pair, quad),
            dst_ref=slot(t, me),
            send_sem=send_sem.at[t, pair * n_quad + quad],
            recv_sem=recv_sem.at[t, me],
            device_id=(slab, pair, quad),
            device_id_type=MESH,
        )

    def place(pair):
        return pair // n_inner - (1 - side) * far, edge_outer * n_inner + pair % n_inner

    def send_to_sum(t, pair, quad):
        at, target = place(pair)
        return pltpu.make_async_remote_copy(
            src_ref=part(t, pair, quad),
            dst_ref=gather_slot(t, at, my_source),
            send_sem=send_sem.at[t, pair * n_quad + quad],
            recv_sem=gather_sem.at[t, at, my_source],
            device_id=(slab, target, quad),
            device_id_type=MESH,
        )

    def smooth(t, pair):
        at_row = pl.multiple_of(pair * rows + t * STRIP, STRIP)
        for l in range(local):
            columns = [smooth_rows(padded.at[l, j], at_row) for j in range(tiles)]
            ready[l, pl.ds(at_row, STRIP), :] = smooth_columns(columns)

    def across(s):
        outer, inner = s // n_inner, (s + my_inner) % n_inner
        return ((1 - side) * (2 * far - 1 - outer) + side * outer) * n_inner + inner

    def produce_raw(i, carry):
        t, pair = i // half_pair, across(i % half_pair)
        smooth(t, pair)
        for j in range(n_quad):
            send(t, pair, (my_quad + j) % n_quad).start()
        return carry

    def produce_summed(i, carry):
        t, pair = raw + i // half_pair, across(i % half_pair)
        smooth(t, pair)
        at, target = place(pair)
        for j in range(1, n_quad):
            send_to_sum(t, pair, (my_quad + j) % n_quad).start()

        @pl.when(target != my_pair)
        def _():
            send_to_sum(t, pair, my_quad).start()

        @pl.when(target == my_pair)
        def _():
            pltpu.make_async_copy(
                part(t, pair, my_quad), gather_slot(t, at, my_source), gather_sem.at[t, at, my_source]
            ).start()

        return carry

    def produce_near(i, carry):
        t, s = i // half_pair, i % half_pair
        pair = side * half_pair + (my_pair + 1 + s) % half_pair
        smooth(t, pair)
        for j in range(1, n_quad):
            send(t, pair, (my_quad + j) % n_quad).start()

        @pl.when(pair != my_pair)
        def _():
            send(t, pair, my_quad).start()

        @pl.when(pair == my_pair)
        def _():
            pltpu.make_async_copy(part(t, my_pair, my_quad), slot(t, me), recv_sem.at[t, me]).start()

        return carry

    def sum_copy(t, at):
        return pltpu.make_async_remote_copy(
            src_ref=summed.at[at, pl.ds(TERMS, E - TERMS), strip_rows(t), :],
            dst_ref=arrived.at[pl.ds(TERMS, E - TERMS), strip_rows(t), :],
            send_sem=sum_send_sem.at[t, at],
            recv_sem=sum_recv_sem.at[t],
            device_id=(slab, ((1 - side) * far + at) * n_inner + my_inner, my_quad),
            device_id_type=MESH,
        )

    def add_up(i, carry):
        t, k = i // far, i % far
        at = (far - 1 - k) * (1 - side) + k * side

        def wait(source, carry):
            pltpu.make_async_copy(
                gather_slot(t, at, source), gather_slot(t, at, source), gather_sem.at[t, at, source]
            ).wait()
            return carry

        lax.fori_loop(0, half_n, wait, 0)
        summed[at, :, strip_rows(t), :] = times_stack(spread[2], gathered[at, :, :, strip_rows(t), :])
        sum_copy(t, at).start()
        return carry

    lax.fori_loop(0, raw * half_pair, produce_raw, 0)
    if raw < strips:
        lax.fori_loop(0, (strips - raw) * half_pair, produce_summed, 0)

    q, v = pair_weights(epochs_ref[...], days_ref[...])
    m = jnp.dot(q, v, precision=HIGHEST, preferred_element_type=jnp.float32)
    count = half_n * local
    spread[0] = spread_weights(m, E + side * count, count)
    spread[1] = spread_weights(m, E + (1 - side) * count, count)
    if raw < strips:
        spread[2] = spread_weights(v, E + side * count, count)
        spread[3] = spread_weights(q, 0, E)

        @pl.when(my_pair // n_inner == edge_outer)
        def _():
            lax.fori_loop(raw * far, (raw + 1) * far, add_up, 0)

    lax.fori_loop(0, strips * half_pair, produce_near, 0)

    if raw < strips:

        @pl.when(my_pair // n_inner == edge_outer)
        def _():
            lax.fori_loop((raw + 1) * far, strips * far, add_up, 0)

    def wait_for(t, first):
        def wait(source, carry):
            pltpu.make_async_copy(slot(t, source), slot(t, source), recv_sem.at[t, source]).wait()
            return carry

        lax.fori_loop(first, first + half_n, wait, 0)

    def out_copy(t):
        return pltpu.make_async_copy(result.at[:, strip_rows(t), :], out_hbm.at[:, strip_rows(t), :], out_sem.at[t])

    def own_side(t, carry):
        wait_for(t, side * half_n)
        stack = held[pl.ds(side * half_n, half_n), :, strip_rows(t), :]
        result[:, strip_rows(t), :] = times_stack(spread[0], stack)
        return carry

    def far_side(t, carry):
        wait_for(t, (1 - side) * half_n)
        stack = held[pl.ds((1 - side) * half_n, half_n), :, strip_rows(t), :]
        result[:, strip_rows(t), :] += times_stack(spread[1], stack)
        out_copy(t).start()
        return carry

    def far_sums(t, carry):
        strip = arrived.at[pl.ds(TERMS, E - TERMS), strip_rows(t), :]
        pltpu.make_async_copy(strip, strip, sum_recv_sem.at[t]).wait()
        result[:, strip_rows(t), :] += times_stack(spread[3], arrived[:, strip_rows(t), :])
        out_copy(t).start()
        return carry

    lax.fori_loop(0, strips, own_side, 0)
    lax.fori_loop(0, raw, far_side, 0)
    if raw < strips:
        lax.fori_loop(raw, strips, far_sums, 0)

    def sent_raw(i, carry):
        t, other = i // half_n, (1 - side) * half_n + i % half_n
        send(t, other // n_quad, other % n_quad).wait_send()
        return carry

    def sent_summed(i, carry):
        t, other = raw + i // half_n, (1 - side) * half_n + i % half_n
        pair, quad = other // n_quad, other % n_quad

        @pl.when(place(pair)[1] * n_quad + quad != me)
        def _():
            send_to_sum(t, pair, quad).wait_send()

        return carry

    def sent_near(i, carry):
        t, other = i // (half_n - 1), side * half_n + (me + 1 + i % (half_n - 1)) % half_n
        send(t, other // n_quad, other % n_quad).wait_send()
        return carry

    def sent_sums(i, carry):
        sum_copy(i // far, i % far).wait_send()
        return carry

    lax.fori_loop(0, raw * half_n, sent_raw, 0)
    lax.fori_loop(0, strips * (half_n - 1), sent_near, 0)
    if raw < strips:
        lax.fori_loop(0, (strips - raw) * half_n, sent_summed, 0)

        @pl.when(my_pair // n_inner == edge_outer)
        def _():
            lax.fori_loop(raw * far, strips * far, sent_sums, 0)

    for t in range(strips):
        out_copy(t).wait()


def shards(n_inner, interferograms, pair_epochs, days):
    n_pair = lax.axis_size("pair")
    n_quad = lax.axis_size("quad")
    n = n_pair * n_quad
    local, height, width = interferograms.shape
    rows, cols = height // n_pair, width // n_quad
    strips = rows // STRIP
    far = n_pair // n_inner // 2
    sums = raw_strips(n_pair // n_inner, strips) < strips
    gathered = (far, n // 2, local, rows, cols) if sums else (1, 1, local, STRIP, LANES)
    summed = (far, E, rows, cols) if sums else (1, E, STRIP, LANES)
    return pl.pallas_call(
        functools.partial(kernel, n_pair, n_quad, n_inner),
        out_shape=jax.ShapeDtypeStruct((E, rows, cols), jnp.float32),
        in_specs=[pl.BlockSpec(memory_space=pl.ANY)] * 3,
        out_specs=pl.BlockSpec(memory_space=pl.ANY),
        scratch_shapes=[
            pltpu.VMEM((local, width // LANES, height + 2 * STRIP, LANES), jnp.float32),
            pltpu.VMEM((local, height, width), jnp.float32),
            pltpu.VMEM((n, local, rows, cols), jnp.float32),
            pltpu.VMEM(gathered, jnp.float32),
            pltpu.VMEM(summed, jnp.float32),
            pltpu.VMEM(summed[1:], jnp.float32),
            pltpu.VMEM((4, E * STRIP, n // 2 * local * STRIP), jnp.float32),
            pltpu.VMEM((E, rows, cols), jnp.float32),
            pltpu.VMEM(pair_epochs.shape, jnp.int32),
            pltpu.VMEM((1,) + days.shape, jnp.int32),
            pltpu.SemaphoreType.DMA((local, width // LANES)),
            pltpu.SemaphoreType.DMA((2,)),
            pltpu.SemaphoreType.DMA((strips, n)),
            pltpu.SemaphoreType.DMA((strips, n)),
            pltpu.SemaphoreType.DMA((strips, far, n // 2) if sums else (1, 1, 1)),
            pltpu.SemaphoreType.DMA((strips, far)),
            pltpu.SemaphoreType.DMA((strips,)),
            pltpu.SemaphoreType.DMA((strips,)),
        ],
        compiler_params=pltpu.CompilerParams(
            collective_id=0, has_side_effects=True, vmem_limit_bytes=48 * 1024 * 1024
        ),
        name="smooth_and_invert",
    )(interferograms, pair_epochs, days[None, :])


def inner_size(mesh):
    line = list(mesh.devices[0, :, 0])
    coords = [getattr(d, "coords", None) for d in line]
    if any(c is None for c in coords):
        return 1
    moving = [k for k in range(len(coords[0])) if coords[0][k] != coords[-1][k]]
    for k in moving:
        run = 1
        while run < len(line) and coords[run][k] == coords[0][k]:
            run += 1
        if 1 < run < len(line) and len(line) % run == 0:
            return run
    return 1


def solution(mesh):
    placed = (P(("pair", "quad"), "slab", None), P(), P())
    return jax.shard_map(
        functools.partial(shards, inner_size(mesh)),
        mesh=mesh,
        in_specs=placed,
        out_specs=P(None, ("slab", "pair"), "quad"),
        check_vma=False,
    )
```

```python
import functools
import math

import jax
import jax.numpy as jnp
from jax import lax
from jax.experimental import pallas as pl
from jax.experimental.pallas import tpu as pltpu
from jax.sharding import PartitionSpec as P

E = 32
RADIUS = 6
STRIP = 8
LANES = 128
MESH = pl.DeviceIdType.MESH
HIGHEST = lax.Precision.HIGHEST
TERMS = 4


def gauss_taps():
    weights = [math.exp(-i * i / 8.0) for i in range(-RADIUS, RADIUS + 1)]
    return [w / sum(weights) for w in weights]


def iota(shape, dim):
    return lax.broadcasted_iota(jnp.int32, shape, dim)


def smooth_rows(column, at_row):
    taps = gauss_taps()
    rows = [column[pl.ds(at_row + STRIP - RADIUS + i, STRIP), :] for i in range(2 * RADIUS + 1)]
    total = taps[RADIUS] * rows[RADIUS]
    for i in range(1, RADIUS + 1):
        total = total + taps[RADIUS + i] * (rows[RADIUS - i] + rows[RADIUS + i])
    return total


def smooth_columns(columns):
    taps = gauss_taps()
    wide = jnp.concatenate(columns + [jnp.zeros_like(columns[0])], axis=1)
    span = wide.shape[1]
    total = taps[RADIUS] * wide
    for i in range(1, RADIUS + 1):
        total = total + taps[RADIUS + i] * (pltpu.roll(wide, i, 1) + pltpu.roll(wide, span - i, 1))
    return total[:, : span - LANES]


def pair_weights(pair_epochs, days):
    pairs = pair_epochs.shape[1]
    first, second = pair_epochs[0:1], pair_epochs[1:2]
    step = iota((E, pairs), 0)
    design_t = jnp.where((first <= step) & (step < second), 1.0, 0.0)
    row, col = iota((LANES, pairs), 0), iota((LANES, pairs), 1)
    inside = (row < E) & (first <= row) & (row < second)
    other = jnp.where(inside | (row == col + E), 1.0, 0.0)
    system = lax.dot_general(
        design_t, other, (((1,), (1,)), ((), ())), precision=HIGHEST, preferred_element_type=jnp.float32
    )
    row, col = iota((E, LANES), 0), iota((E, LANES), 1)
    system = system + jnp.where((row == E - 1) & (col == E - 1), 1.0, 0.0)

    def eliminate(k, a):
        pivot_row = jnp.sum(jnp.where(row == k, a, 0.0), axis=0, keepdims=True)
        pivot_col = jnp.sum(jnp.where(col == k, a, 0.0), axis=1, keepdims=True)
        pivot = jnp.sum(jnp.where(row[:, 0:1] == k, pivot_col, 0.0), axis=0, keepdims=True)
        scaled = pivot_row / pivot
        return jnp.where(row == k, scaled, a - pivot_col * scaled)

    system = lax.fori_loop(0, E, eliminate, system)

    times = days.astype(jnp.float32)
    centred = (times - jnp.sum(times, axis=1, keepdims=True) / E) / 365.25
    phase = 2.0 * math.pi * times / 365.25
    erow, ecol = iota((E, E), 0), iota((E, E), 1)
    lane = ecol[0:1]
    eye = jnp.where(erow == ecol, 1.0, 0.0)
    q, q_t = eye, eye
    columns = [jnp.ones_like(times), centred, jnp.sin(phase), jnp.cos(phase)]
    for j in range(TERMS):
        below = jnp.where(lane >= j, columns[j], 0.0)
        head = jnp.sum(jnp.where(lane == j, below, 0.0), axis=1, keepdims=True)
        norm = jnp.sqrt(jnp.sum(below * below, axis=1, keepdims=True))
        v = below + jnp.where(lane == j, jnp.where(head >= 0, norm, -norm), 0.0)
        v = v * lax.rsqrt(0.5 * jnp.sum(v * v, axis=1, keepdims=True))
        upright = jnp.sum(jnp.where(erow == ecol, v, 0.0), axis=1, keepdims=True)
        columns = [c - v * jnp.sum(v * c, axis=1, keepdims=True) for c in columns]
        q = q - jnp.sum(q * v, axis=1, keepdims=True) * v
        q_t = q_t - upright * jnp.sum(q_t * upright, axis=0, keepdims=True)
    q = jnp.where(ecol >= TERMS, q, 0.0)
    q_t = jnp.where(erow >= TERMS, q_t, 0.0)
    summing = jnp.where(ecol < erow, 1.0, 0.0)
    displacement = jnp.dot(summing, system, precision=HIGHEST, preferred_element_type=jnp.float32)
    return q, jnp.dot(q_t, displacement, precision=HIGHEST, preferred_element_type=jnp.float32)


def spread_weights(weights, first, count):
    tall, wide, depth = E * STRIP, count * STRIP, weights.shape[1]
    right = jnp.where(iota((depth, wide), 0) == iota((depth, wide), 1) // STRIP + first, 1.0, 0.0)
    left = jnp.where(iota((tall, E), 1) == iota((tall, E), 0) // STRIP, 1.0, 0.0)
    full = jnp.dot(weights, right, precision=HIGHEST, preferred_element_type=jnp.float32)
    full = jnp.dot(left, full, precision=HIGHEST, preferred_element_type=jnp.float32)
    same = iota((tall, wide), 0) % STRIP == iota((tall, wide), 1) % STRIP
    return jnp.where(same, full, 0.0)


def times_stack(weights, stack):
    flat = stack.reshape(weights.shape[1], stack.shape[-1])
    total = jnp.dot(weights, flat, precision=HIGHEST, preferred_element_type=jnp.float32)
    return total.reshape(E, STRIP, stack.shape[-1])


def raw_strips(n_outer, strips):
    return 1 if n_outer > 1 and n_outer // 2 <= 2 else strips


def kernel(
    n_pair, n_quad, n_inner,
    x_hbm, epochs_hbm, days_hbm, out_hbm,
    padded, ready, held, gathered, summed, arrived, spread, result, epochs_ref, days_ref,
    in_sem, small_sem, send_sem, recv_sem, gather_sem, sum_send_sem, sum_recv_sem, out_sem,
):
    local, height, width = ready.shape
    n = n_pair * n_quad
    n_outer = n_pair // n_inner
    half_n, half_pair = n // 2, n_pair // 2
    far = n_outer // 2
    rows, cols = height // n_pair, width // n_quad
    strips = rows // STRIP
    raw = raw_strips(n_outer, strips)
    tiles = width // LANES
    slab = lax.axis_index("slab")
    my_pair = lax.axis_index("pair")
    my_quad = lax.axis_index("quad")
    me = my_pair * n_quad + my_quad
    side = my_pair // half_pair
    my_source = me % half_n
    my_inner = my_pair % n_inner
    edge_outer = far - 1 + side

    loads = [
        pltpu.make_async_copy(
            x_hbm.at[l, :, pl.ds(j * LANES, LANES)],
            padded.at[l, j, pl.ds(STRIP, height), :],
            in_sem.at[l, j],
        )
        for l in range(local)
        for j in range(tiles)
    ]
    loads += [
        pltpu.make_async_copy(epochs_hbm, epochs_ref, small_sem.at[0]),
        pltpu.make_async_copy(days_hbm, days_ref, small_sem.at[1]),
    ]
    for load in loads:
        load.start()
    barrier = pltpu.get_barrier_semaphore()

    def greet(j, carry):
        other = lax.rem(me + j, n)
        pl.semaphore_signal(
            barrier, inc=1, device_id=(slab, other // n_quad, other % n_quad), device_id_type=MESH
        )
        return carry

    lax.fori_loop(1, n, greet, 0)
    edge = jnp.zeros((local, tiles, STRIP, LANES), jnp.float32)
    padded[:, :, 0:STRIP, :] = edge
    padded[:, :, STRIP + height : 2 * STRIP + height, :] = edge
    if raw < strips:
        arrived[0:TERMS] = jnp.zeros((TERMS, rows, cols), jnp.float32)
    for load in loads:
        load.wait()
    pl.semaphore_wait(barrier, n - 1)

    def strip_rows(t):
        return pl.ds(pl.multiple_of(t * STRIP, STRIP), STRIP)

    def part(t, pair, quad):
        at_row = pl.multiple_of(pair * rows + t * STRIP, STRIP)
        at_col = pl.multiple_of(quad * cols, LANES)
        return ready.at[:, pl.ds(at_row, STRIP), pl.ds(at_col, cols)]

    def slot(t, source):
        return held.at[source, :, strip_rows(t), :]

    def gather_slot(t, at, source):
        return gathered.at[at, source, :, strip_rows(t), :]

    def send(t, pair, quad):
        return pltpu.make_async_remote_copy(
            src_ref=part(t, pair, quad),
            dst_ref=slot(t, me),
            send_sem=send_sem.at[t, pair * n_quad + quad],
            recv_sem=recv_sem.at[t, me],
            device_id=(slab, pair, quad),
            device_id_type=MESH,
        )

    def place(pair):
        return pair // n_inner - (1 - side) * far, edge_outer * n_inner + pair % n_inner

    def send_to_sum(t, pair, quad):
        at, target = place(pair)
        return pltpu.make_async_remote_copy(
            src_ref=part(t, pair, quad),
            dst_ref=gather_slot(t, at, my_source),
            send_sem=send_sem.at[t, pair * n_quad + quad],
            recv_sem=gather_sem.at[t, at, my_source],
            device_id=(slab, target, quad),
            device_id_type=MESH,
        )

    def smooth(t, pair):
        at_row = pl.multiple_of(pair * rows + t * STRIP, STRIP)
        for l in range(local):
            columns = [smooth_rows(padded.at[l, j], at_row) for j in range(tiles)]
            ready[l, pl.ds(at_row, STRIP), :] = smooth_columns(columns)

    def across(s):
        outer, inner = s // n_inner, (s + my_inner) % n_inner
        return ((1 - side) * (2 * far - 1 - outer) + side * outer) * n_inner + inner

    def produce_raw(i, carry):
        t, pair = i // half_pair, across(i % half_pair)
        smooth(t, pair)
        for j in range(n_quad):
            send(t, pair, (my_quad + j) % n_quad).start()
        return carry

    def produce_summed(i, carry):
        t, pair = raw + i // half_pair, across(i % half_pair)
        smooth(t, pair)
        at, target = place(pair)
        for j in range(1, n_quad):
            send_to_sum(t, pair, (my_quad + j) % n_quad).start()

        @pl.when(target != my_pair)
        def _():
            send_to_sum(t, pair, my_quad).start()

        @pl.when(target == my_pair)
        def _():
            pltpu.make_async_copy(
                part(t, pair, my_quad), gather_slot(t, at, my_source), gather_sem.at[t, at, my_source]
            ).start()

        return carry

    def produce_near(i, carry):
        t, s = i // half_pair, i % half_pair
        pair = side * half_pair + (my_pair + 1 + s) % half_pair
        smooth(t, pair)
        for j in range(1, n_quad):
            send(t, pair, (my_quad + j) % n_quad).start()

        @pl.when(pair != my_pair)
        def _():
            send(t, pair, my_quad).start()

        @pl.when(pair == my_pair)
        def _():
            pltpu.make_async_copy(part(t, my_pair, my_quad), slot(t, me), recv_sem.at[t, me]).start()

        return carry

    def sum_copy(t, at):
        return pltpu.make_async_remote_copy(
            src_ref=summed.at[at, pl.ds(TERMS, E - TERMS), strip_rows(t), :],
            dst_ref=arrived.at[pl.ds(TERMS, E - TERMS), strip_rows(t), :],
            send_sem=sum_send_sem.at[t, at],
            recv_sem=sum_recv_sem.at[t],
            device_id=(slab, ((1 - side) * far + at) * n_inner + my_inner, my_quad),
            device_id_type=MESH,
        )

    def add_up(i, carry):
        t, k = i // far, i % far
        at = (far - 1 - k) * (1 - side) + k * side

        def wait(source, carry):
            pltpu.make_async_copy(
                gather_slot(t, at, source), gather_slot(t, at, source), gather_sem.at[t, at, source]
            ).wait()
            return carry

        lax.fori_loop(0, half_n, wait, 0)
        summed[at, :, strip_rows(t), :] = times_stack(spread[2], gathered[at, :, :, strip_rows(t), :])
        sum_copy(t, at).start()
        return carry

    split = min(raw + 1, strips)
    lax.fori_loop(0, raw * half_pair, produce_raw, 0)
    lax.fori_loop(0, (split - raw) * half_pair, produce_summed, 0)

    q, v = pair_weights(epochs_ref[...], days_ref[...])
    m = jnp.dot(q, v, precision=HIGHEST, preferred_element_type=jnp.float32)
    count = half_n * local
    spread[0] = spread_weights(m, E + side * count, count)
    spread[1] = spread_weights(m, E + (1 - side) * count, count)
    if raw < strips:
        spread[2] = spread_weights(v, E + side * count, count)
        spread[3] = spread_weights(q, 0, E)

    lax.fori_loop((split - raw) * half_pair, (strips - raw) * half_pair, produce_summed, 0)
    early = strips // 2 if raw < strips else strips
    lax.fori_loop(0, early * half_pair, produce_near, 0)

    if raw < strips:

        @pl.when(my_pair // n_inner == edge_outer)
        def _():
            lax.fori_loop(raw * far, split * far, add_up, 0)

        lax.fori_loop(early * half_pair, strips * half_pair, produce_near, 0)

        @pl.when(my_pair // n_inner == edge_outer)
        def _():
            lax.fori_loop(split * far, strips * far, add_up, 0)

    def wait_for(t, first):
        def wait(source, carry):
            pltpu.make_async_copy(slot(t, source), slot(t, source), recv_sem.at[t, source]).wait()
            return carry

        lax.fori_loop(first, first + half_n, wait, 0)

    def out_copy(t):
        return pltpu.make_async_copy(result.at[:, strip_rows(t), :], out_hbm.at[:, strip_rows(t), :], out_sem.at[t])

    def own_side(t, carry):
        wait_for(t, side * half_n)
        stack = held[pl.ds(side * half_n, half_n), :, strip_rows(t), :]
        result[:, strip_rows(t), :] = times_stack(spread[0], stack)
        return carry

    def far_side(t, carry):
        wait_for(t, (1 - side) * half_n)
        stack = held[pl.ds((1 - side) * half_n, half_n), :, strip_rows(t), :]
        result[:, strip_rows(t), :] += times_stack(spread[1], stack)
        out_copy(t).start()
        return carry

    def far_sums(t, carry):
        strip = arrived.at[pl.ds(TERMS, E - TERMS), strip_rows(t), :]
        pltpu.make_async_copy(strip, strip, sum_recv_sem.at[t]).wait()
        result[:, strip_rows(t), :] += times_stack(spread[3], arrived[:, strip_rows(t), :])
        out_copy(t).start()
        return carry

    lax.fori_loop(0, strips, own_side, 0)
    lax.fori_loop(0, raw, far_side, 0)
    if raw < strips:
        lax.fori_loop(raw, strips, far_sums, 0)

    def sent_raw(i, carry):
        t, other = i // half_n, (1 - side) * half_n + i % half_n
        send(t, other // n_quad, other % n_quad).wait_send()
        return carry

    def sent_summed(i, carry):
        t, other = raw + i // half_n, (1 - side) * half_n + i % half_n
        pair, quad = other // n_quad, other % n_quad

        @pl.when(place(pair)[1] * n_quad + quad != me)
        def _():
            send_to_sum(t, pair, quad).wait_send()

        return carry

    def sent_near(i, carry):
        t, other = i // (half_n - 1), side * half_n + (me + 1 + i % (half_n - 1)) % half_n
        send(t, other // n_quad, other % n_quad).wait_send()
        return carry

    def sent_sums(i, carry):
        sum_copy(i // far, i % far).wait_send()
        return carry

    lax.fori_loop(0, raw * half_n, sent_raw, 0)
    lax.fori_loop(0, strips * (half_n - 1), sent_near, 0)
    if raw < strips:
        lax.fori_loop(0, (strips - raw) * half_n, sent_summed, 0)

        @pl.when(my_pair // n_inner == edge_outer)
        def _():
            lax.fori_loop(raw * far, strips * far, sent_sums, 0)

    for t in range(strips):
        out_copy(t).wait()


def shards(n_inner, interferograms, pair_epochs, days):
    n_pair = lax.axis_size("pair")
    n_quad = lax.axis_size("quad")
    n = n_pair * n_quad
    local, height, width = interferograms.shape
    rows, cols = height // n_pair, width // n_quad
    strips = rows // STRIP
    far = n_pair // n_inner // 2
    sums = raw_strips(n_pair // n_inner, strips) < strips
    gathered = (far, n // 2, local, rows, cols) if sums else (1, 1, local, STRIP, LANES)
    summed = (far, E, rows, cols) if sums else (1, E, STRIP, LANES)
    return pl.pallas_call(
        functools.partial(kernel, n_pair, n_quad, n_inner),
        out_shape=jax.ShapeDtypeStruct((E, rows, cols), jnp.float32),
        in_specs=[pl.BlockSpec(memory_space=pltpu.HBM)] * 3,
        out_specs=pl.BlockSpec(memory_space=pl.ANY),
        scratch_shapes=[
            pltpu.VMEM((local, width // LANES, height + 2 * STRIP, LANES), jnp.float32),
            pltpu.VMEM((local, height, width), jnp.float32),
            pltpu.VMEM((n, local, rows, cols), jnp.float32),
            pltpu.VMEM(gathered, jnp.float32),
            pltpu.VMEM(summed, jnp.float32),
            pltpu.VMEM(summed[1:], jnp.float32),
            pltpu.VMEM((4, E * STRIP, n // 2 * local * STRIP), jnp.float32),
            pltpu.VMEM((E, rows, cols), jnp.float32),
            pltpu.VMEM(pair_epochs.shape, jnp.int32),
            pltpu.VMEM((1,) + days.shape, jnp.int32),
            pltpu.SemaphoreType.DMA((local, width // LANES)),
            pltpu.SemaphoreType.DMA((2,)),
            pltpu.SemaphoreType.DMA((strips, n)),
            pltpu.SemaphoreType.DMA((strips, n)),
            pltpu.SemaphoreType.DMA((strips, far, n // 2) if sums else (1, 1, 1)),
            pltpu.SemaphoreType.DMA((strips, far)),
            pltpu.SemaphoreType.DMA((strips,)),
            pltpu.SemaphoreType.DMA((strips,)),
        ],
        compiler_params=pltpu.CompilerParams(
            collective_id=0, has_side_effects=True, vmem_limit_bytes=63 * 1024 * 1024
        ),
        name="smooth_and_invert",
    )(interferograms, pair_epochs, days[None, :])


def inner_size(mesh):
    line = list(mesh.devices[0, :, 0])
    coords = [getattr(d, "coords", None) for d in line]
    if any(c is None for c in coords):
        return 1
    moving = [k for k in range(len(coords[0])) if coords[0][k] != coords[-1][k]]
    for k in moving:
        run = 1
        while run < len(line) and coords[run][k] == coords[0][k]:
            run += 1
        if 1 < run < len(line) and len(line) % run == 0:
            return run
    return 1


def solution(mesh):
    placed = (P(("pair", "quad"), "slab", None), P(), P())
    return jax.shard_map(
        functools.partial(shards, inner_size(mesh)),
        mesh=mesh,
        in_specs=placed,
        out_specs=P(None, ("slab", "pair"), "quad"),
        check_vma=False,
    )
```

```python
import functools
import math

import jax
import jax.numpy as jnp
from jax import lax
from jax.experimental import pallas as pl
from jax.experimental.pallas import tpu as pltpu
from jax.sharding import PartitionSpec as P

E = 32
RADIUS = 6
STRIP = 8
LANES = 128
MESH = pl.DeviceIdType.MESH
HIGHEST = lax.Precision.HIGHEST
TERMS = 4


def gauss_taps():
    weights = [math.exp(-i * i / 8.0) for i in range(-RADIUS, RADIUS + 1)]
    return [w / sum(weights) for w in weights]


def iota(shape, dim):
    return lax.broadcasted_iota(jnp.int32, shape, dim)


def smooth_rows(column, at_row):
    taps = gauss_taps()
    rows = [column[pl.ds(at_row + STRIP - RADIUS + i, STRIP), :] for i in range(2 * RADIUS + 1)]
    total = taps[RADIUS] * rows[RADIUS]
    for i in range(1, RADIUS + 1):
        total = total + taps[RADIUS + i] * (rows[RADIUS - i] + rows[RADIUS + i])
    return total


def smooth_columns(columns):
    taps = gauss_taps()
    wide = jnp.concatenate(columns + [jnp.zeros_like(columns[0])], axis=1)
    span = wide.shape[1]
    total = taps[RADIUS] * wide
    for i in range(1, RADIUS + 1):
        total = total + taps[RADIUS + i] * (pltpu.roll(wide, i, 1) + pltpu.roll(wide, span - i, 1))
    return total[:, : span - LANES]


def pair_weights(pair_epochs, days):
    pairs = pair_epochs.shape[1]
    first, second = pair_epochs[0:1], pair_epochs[1:2]
    step = iota((E, pairs), 0)
    design_t = jnp.where((first <= step) & (step < second), 1.0, 0.0)
    row, col = iota((LANES, pairs), 0), iota((LANES, pairs), 1)
    inside = (row < E) & (first <= row) & (row < second)
    other = jnp.where(inside | (row == col + E), 1.0, 0.0)
    system = lax.dot_general(
        design_t, other, (((1,), (1,)), ((), ())), precision=HIGHEST, preferred_element_type=jnp.float32
    )
    row, col = iota((E, LANES), 0), iota((E, LANES), 1)
    system = system + jnp.where((row == E - 1) & (col == E - 1), 1.0, 0.0)

    def eliminate(k, a):
        pivot_row = jnp.sum(jnp.where(row == k, a, 0.0), axis=0, keepdims=True)
        pivot_col = jnp.sum(jnp.where(col == k, a, 0.0), axis=1, keepdims=True)
        pivot = jnp.sum(jnp.where(row[:, 0:1] == k, pivot_col, 0.0), axis=0, keepdims=True)
        scaled = pivot_row / pivot
        return jnp.where(row == k, scaled, a - pivot_col * scaled)

    system = lax.fori_loop(0, E, eliminate, system)

    times = days.astype(jnp.float32)
    centred = (times - jnp.sum(times, axis=1, keepdims=True) / E) / 365.25
    phase = 2.0 * math.pi * times / 365.25
    erow, ecol = iota((E, E), 0), iota((E, E), 1)
    lane = ecol[0:1]
    eye = jnp.where(erow == ecol, 1.0, 0.0)
    q, q_t = eye, eye
    columns = [jnp.ones_like(times), centred, jnp.sin(phase), jnp.cos(phase)]
    for j in range(TERMS):
        below = jnp.where(lane >= j, columns[j], 0.0)
        head = jnp.sum(jnp.where(lane == j, below, 0.0), axis=1, keepdims=True)
        norm = jnp.sqrt(jnp.sum(below * below, axis=1, keepdims=True))
        v = below + jnp.where(lane == j, jnp.where(head >= 0, norm, -norm), 0.0)
        v = v * lax.rsqrt(0.5 * jnp.sum(v * v, axis=1, keepdims=True))
        upright = jnp.sum(jnp.where(erow == ecol, v, 0.0), axis=1, keepdims=True)
        columns = [c - v * jnp.sum(v * c, axis=1, keepdims=True) for c in columns]
        q = q - jnp.sum(q * v, axis=1, keepdims=True) * v
        q_t = q_t - upright * jnp.sum(q_t * upright, axis=0, keepdims=True)
    q = jnp.where(ecol >= TERMS, q, 0.0)
    q_t = jnp.where(erow >= TERMS, q_t, 0.0)
    summing = jnp.where(ecol < erow, 1.0, 0.0)
    displacement = jnp.dot(summing, system, precision=HIGHEST, preferred_element_type=jnp.float32)
    return q, jnp.dot(q_t, displacement, precision=HIGHEST, preferred_element_type=jnp.float32)


def spread_weights(weights, first, count):
    tall, wide, depth = E * STRIP, count * STRIP, weights.shape[1]
    right = jnp.where(iota((depth, wide), 0) == iota((depth, wide), 1) // STRIP + first, 1.0, 0.0)
    left = jnp.where(iota((tall, E), 1) == iota((tall, E), 0) // STRIP, 1.0, 0.0)
    full = jnp.dot(weights, right, precision=HIGHEST, preferred_element_type=jnp.float32)
    full = jnp.dot(left, full, precision=HIGHEST, preferred_element_type=jnp.float32)
    same = iota((tall, wide), 0) % STRIP == iota((tall, wide), 1) % STRIP
    return jnp.where(same, full, 0.0)


def times_stack(weights, stack):
    flat = stack.reshape(weights.shape[1], stack.shape[-1])
    total = jnp.dot(weights, flat, precision=HIGHEST, preferred_element_type=jnp.float32)
    return total.reshape(E, STRIP, stack.shape[-1])


def raw_strips(n_outer, strips):
    return strips // 2 if n_outer > 1 and n_outer // 2 <= 2 else strips


def kernel(
    n_pair, n_quad, n_inner,
    x_hbm, epochs_hbm, days_hbm, out_hbm,
    padded, ready, held, gathered, summed, arrived, spread, result, epochs_ref, days_ref,
    in_sem, small_sem, send_sem, recv_sem, gather_sem, sum_send_sem, sum_recv_sem, out_sem,
):
    local, height, width = ready.shape
    n = n_pair * n_quad
    n_outer = n_pair // n_inner
    half_n, half_pair = n // 2, n_pair // 2
    far = n_outer // 2
    rows, cols = height // n_pair, width // n_quad
    strips = rows // STRIP
    raw = raw_strips(n_outer, strips)
    tiles = width // LANES
    slab = lax.axis_index("slab")
    my_pair = lax.axis_index("pair")
    my_quad = lax.axis_index("quad")
    me = my_pair * n_quad + my_quad
    side = my_pair // half_pair
    my_source = me % half_n
    my_inner = my_pair % n_inner
    edge_outer = far - 1 + side

    loads = [
        pltpu.make_async_copy(
            x_hbm.at[l, :, pl.ds(j * LANES, LANES)],
            padded.at[l, j, pl.ds(STRIP, height), :],
            in_sem.at[l, j],
        )
        for l in range(local)
        for j in range(tiles)
    ]
    loads += [
        pltpu.make_async_copy(epochs_hbm, epochs_ref, small_sem.at[0]),
        pltpu.make_async_copy(days_hbm, days_ref, small_sem.at[1]),
    ]
    for load in loads:
        load.start()
    barrier = pltpu.get_barrier_semaphore()

    def greet(j, carry):
        other = lax.rem(me + j, n)
        pl.semaphore_signal(
            barrier, inc=1, device_id=(slab, other // n_quad, other % n_quad), device_id_type=MESH
        )
        return carry

    lax.fori_loop(1, n, greet, 0)
    edge = jnp.zeros((local, tiles, STRIP, LANES), jnp.float32)
    padded[:, :, 0:STRIP, :] = edge
    padded[:, :, STRIP + height : 2 * STRIP + height, :] = edge
    if raw < strips:
        arrived[0:TERMS] = jnp.zeros((TERMS, rows, cols), jnp.float32)
    for load in loads:
        load.wait()
    pl.semaphore_wait(barrier, n - 1)

    def strip_rows(t):
        return pl.ds(pl.multiple_of(t * STRIP, STRIP), STRIP)

    def part(t, pair, quad):
        at_row = pl.multiple_of(pair * rows + t * STRIP, STRIP)
        at_col = pl.multiple_of(quad * cols, LANES)
        return ready.at[:, pl.ds(at_row, STRIP), pl.ds(at_col, cols)]

    def slot(t, source):
        return held.at[source, :, strip_rows(t), :]

    def gather_slot(t, at, source):
        return gathered.at[at, source, :, strip_rows(t), :]

    def send(t, pair, quad):
        return pltpu.make_async_remote_copy(
            src_ref=part(t, pair, quad),
            dst_ref=slot(t, me),
            send_sem=send_sem.at[t, pair * n_quad + quad],
            recv_sem=recv_sem.at[t, me],
            device_id=(slab, pair, quad),
            device_id_type=MESH,
        )

    def place(pair):
        return pair // n_inner - (1 - side) * far, edge_outer * n_inner + pair % n_inner

    def send_to_sum(t, pair, quad):
        at, target = place(pair)
        return pltpu.make_async_remote_copy(
            src_ref=part(t, pair, quad),
            dst_ref=gather_slot(t, at, my_source),
            send_sem=send_sem.at[t, pair * n_quad + quad],
            recv_sem=gather_sem.at[t, at, my_source],
            device_id=(slab, target, quad),
            device_id_type=MESH,
        )

    def smooth(t, pair):
        at_row = pl.multiple_of(pair * rows + t * STRIP, STRIP)
        for l in range(local):
            columns = [smooth_rows(padded.at[l, j], at_row) for j in range(tiles)]
            ready[l, pl.ds(at_row, STRIP), :] = smooth_columns(columns)

    def across(s):
        outer, inner = s // n_inner, (s + my_inner) % n_inner
        return ((1 - side) * (2 * far - 1 - outer) + side * outer) * n_inner + inner

    def produce_raw(i, carry):
        t, pair = i // half_pair, across(i % half_pair)
        smooth(t, pair)
        for j in range(n_quad):
            send(t, pair, (my_quad + j) % n_quad).start()
        return carry

    def produce_summed(i, carry):
        t, pair = raw + i // half_pair, across(i % half_pair)
        smooth(t, pair)
        at, target = place(pair)
        for j in range(1, n_quad):
            send_to_sum(t, pair, (my_quad + j) % n_quad).start()

        @pl.when(target != my_pair)
        def _():
            send_to_sum(t, pair, my_quad).start()

        @pl.when(target == my_pair)
        def _():
            pltpu.make_async_copy(
                part(t, pair, my_quad), gather_slot(t, at, my_source), gather_sem.at[t, at, my_source]
            ).start()

        return carry

    def produce_near(i, carry):
        t, s = i // half_pair, i % half_pair
        pair = side * half_pair + (my_pair + 1 + s) % half_pair
        smooth(t, pair)
        for j in range(1, n_quad):
            send(t, pair, (my_quad + j) % n_quad).start()

        @pl.when(pair != my_pair)
        def _():
            send(t, pair, my_quad).start()

        @pl.when(pair == my_pair)
        def _():
            pltpu.make_async_copy(part(t, my_pair, my_quad), slot(t, me), recv_sem.at[t, me]).start()

        return carry

    def sum_copy(t, at):
        return pltpu.make_async_remote_copy(
            src_ref=summed.at[at, pl.ds(TERMS, E - TERMS), strip_rows(t), :],
            dst_ref=arrived.at[pl.ds(TERMS, E - TERMS), strip_rows(t), :],
            send_sem=sum_send_sem.at[t, at],
            recv_sem=sum_recv_sem.at[t],
            device_id=(slab, ((1 - side) * far + at) * n_inner + my_inner, my_quad),
            device_id_type=MESH,
        )

    def add_up(i, carry):
        t, k = i // far, i % far
        at = (far - 1 - k) * (1 - side) + k * side

        def wait(source, carry):
            pltpu.make_async_copy(
                gather_slot(t, at, source), gather_slot(t, at, source), gather_sem.at[t, at, source]
            ).wait()
            return carry

        lax.fori_loop(0, half_n, wait, 0)
        summed[at, :, strip_rows(t), :] = times_stack(spread[2], gathered[at, :, :, strip_rows(t), :])
        sum_copy(t, at).start()
        return carry

    split = min(raw + 1, strips)
    lax.fori_loop(0, raw * half_pair, produce_raw, 0)
    lax.fori_loop(0, (split - raw) * half_pair, produce_summed, 0)

    q, v = pair_weights(epochs_ref[...], days_ref[...])
    m = jnp.dot(q, v, precision=HIGHEST, preferred_element_type=jnp.float32)
    count = half_n * local
    spread[0] = spread_weights(m, E + side * count, count)
    spread[1] = spread_weights(m, E + (1 - side) * count, count)
    if raw < strips:
        spread[2] = spread_weights(v, E + side * count, count)
        spread[3] = spread_weights(q, 0, E)

    lax.fori_loop((split - raw) * half_pair, (strips - raw) * half_pair, produce_summed, 0)
    early = strips // 2 if raw < strips else strips
    lax.fori_loop(0, early * half_pair, produce_near, 0)

    if raw < strips:

        @pl.when(my_pair // n_inner == edge_outer)
        def _():
            lax.fori_loop(raw * far, split * far, add_up, 0)

        lax.fori_loop(early * half_pair, strips * half_pair, produce_near, 0)

        @pl.when(my_pair // n_inner == edge_outer)
        def _():
            lax.fori_loop(split * far, strips * far, add_up, 0)

    def wait_for(t, first):
        def wait(source, carry):
            pltpu.make_async_copy(slot(t, source), slot(t, source), recv_sem.at[t, source]).wait()
            return carry

        lax.fori_loop(first, first + half_n, wait, 0)

    def out_copy(t):
        return pltpu.make_async_copy(result.at[:, strip_rows(t), :], out_hbm.at[:, strip_rows(t), :], out_sem.at[t])

    def own_side(t, carry):
        wait_for(t, side * half_n)
        stack = held[pl.ds(side * half_n, half_n), :, strip_rows(t), :]
        result[:, strip_rows(t), :] = times_stack(spread[0], stack)
        return carry

    def far_side(t, carry):
        wait_for(t, (1 - side) * half_n)
        stack = held[pl.ds((1 - side) * half_n, half_n), :, strip_rows(t), :]
        result[:, strip_rows(t), :] += times_stack(spread[1], stack)
        out_copy(t).start()
        return carry

    def far_sums(t, carry):
        strip = arrived.at[pl.ds(TERMS, E - TERMS), strip_rows(t), :]
        pltpu.make_async_copy(strip, strip, sum_recv_sem.at[t]).wait()
        result[:, strip_rows(t), :] += times_stack(spread[3], arrived[:, strip_rows(t), :])
        out_copy(t).start()
        return carry

    lax.fori_loop(0, strips, own_side, 0)
    lax.fori_loop(0, raw, far_side, 0)
    if raw < strips:
        lax.fori_loop(raw, strips, far_sums, 0)

    def sent_raw(i, carry):
        t, other = i // half_n, (1 - side) * half_n + i % half_n
        send(t, other // n_quad, other % n_quad).wait_send()
        return carry

    def sent_summed(i, carry):
        t, other = raw + i // half_n, (1 - side) * half_n + i % half_n
        pair, quad = other // n_quad, other % n_quad

        @pl.when(place(pair)[1] * n_quad + quad != me)
        def _():
            send_to_sum(t, pair, quad).wait_send()

        return carry

    def sent_near(i, carry):
        t, other = i // (half_n - 1), side * half_n + (me + 1 + i % (half_n - 1)) % half_n
        send(t, other // n_quad, other % n_quad).wait_send()
        return carry

    def sent_sums(i, carry):
        sum_copy(i // far, i % far).wait_send()
        return carry

    lax.fori_loop(0, raw * half_n, sent_raw, 0)
    lax.fori_loop(0, strips * (half_n - 1), sent_near, 0)
    if raw < strips:
        lax.fori_loop(0, (strips - raw) * half_n, sent_summed, 0)

        @pl.when(my_pair // n_inner == edge_outer)
        def _():
            lax.fori_loop(raw * far, strips * far, sent_sums, 0)

    for t in range(strips):
        out_copy(t).wait()


def shards(n_inner, interferograms, pair_epochs, days):
    n_pair = lax.axis_size("pair")
    n_quad = lax.axis_size("quad")
    n = n_pair * n_quad
    local, height, width = interferograms.shape
    rows, cols = height // n_pair, width // n_quad
    strips = rows // STRIP
    far = n_pair // n_inner // 2
    sums = raw_strips(n_pair // n_inner, strips) < strips
    gathered = (far, n // 2, local, rows, cols) if sums else (1, 1, local, STRIP, LANES)
    summed = (far, E, rows, cols) if sums else (1, E, STRIP, LANES)
    return pl.pallas_call(
        functools.partial(kernel, n_pair, n_quad, n_inner),
        out_shape=jax.ShapeDtypeStruct((E, rows, cols), jnp.float32),
        in_specs=[pl.BlockSpec(memory_space=pltpu.HBM)] * 3,
        out_specs=pl.BlockSpec(memory_space=pl.ANY),
        scratch_shapes=[
            pltpu.VMEM((local, width // LANES, height + 2 * STRIP, LANES), jnp.float32),
            pltpu.VMEM((local, height, width), jnp.float32),
            pltpu.VMEM((n, local, rows, cols), jnp.float32),
            pltpu.VMEM(gathered, jnp.float32),
            pltpu.VMEM(summed, jnp.float32),
            pltpu.VMEM(summed[1:], jnp.float32),
            pltpu.VMEM((4, E * STRIP, n // 2 * local * STRIP), jnp.float32),
            pltpu.VMEM((E, rows, cols), jnp.float32),
            pltpu.VMEM(pair_epochs.shape, jnp.int32),
            pltpu.VMEM((1,) + days.shape, jnp.int32),
            pltpu.SemaphoreType.DMA((local, width // LANES)),
            pltpu.SemaphoreType.DMA((2,)),
            pltpu.SemaphoreType.DMA((strips, n)),
            pltpu.SemaphoreType.DMA((strips, n)),
            pltpu.SemaphoreType.DMA((strips, far, n // 2) if sums else (1, 1, 1)),
            pltpu.SemaphoreType.DMA((strips, far)),
            pltpu.SemaphoreType.DMA((strips,)),
            pltpu.SemaphoreType.DMA((strips,)),
        ],
        compiler_params=pltpu.CompilerParams(
            collective_id=0, has_side_effects=True, vmem_limit_bytes=48 * 1024 * 1024
        ),
        name="smooth_and_invert",
    )(interferograms, pair_epochs, days[None, :])


def inner_size(mesh):
    line = list(mesh.devices[0, :, 0])
    coords = [getattr(d, "coords", None) for d in line]
    if any(c is None for c in coords):
        return 1
    moving = [k for k in range(len(coords[0])) if coords[0][k] != coords[-1][k]]
    for k in moving:
        run = 1
        while run < len(line) and coords[run][k] == coords[0][k]:
            run += 1
        if 1 < run < len(line) and len(line) % run == 0:
            return run
    return 1


def solution(mesh):
    placed = (P(("pair", "quad"), "slab", None), P(), P())
    return jax.shard_map(
        functools.partial(shards, inner_size(mesh)),
        mesh=mesh,
        in_specs=placed,
        out_specs=P(None, ("slab", "pair"), "quad"),
        check_vma=False,
    )
```

```python
import functools
import math

import jax
import jax.numpy as jnp
from jax import lax
from jax.experimental import pallas as pl
from jax.experimental.pallas import tpu as pltpu
from jax.sharding import PartitionSpec as P

E = 32
RADIUS = 6
STRIP = 8
LANES = 128
MESH = pl.DeviceIdType.MESH
HIGHEST = lax.Precision.HIGHEST
TERMS = 4


def gauss_taps():
    weights = [math.exp(-i * i / 8.0) for i in range(-RADIUS, RADIUS + 1)]
    return [w / sum(weights) for w in weights]


def iota(shape, dim):
    return lax.broadcasted_iota(jnp.int32, shape, dim)


def smooth_rows(column, at_row):
    taps = gauss_taps()
    rows = [column[pl.ds(at_row + STRIP - RADIUS + i, STRIP), :] for i in range(2 * RADIUS + 1)]
    total = taps[RADIUS] * rows[RADIUS]
    for i in range(1, RADIUS + 1):
        total = total + taps[RADIUS + i] * (rows[RADIUS - i] + rows[RADIUS + i])
    return total


def smooth_columns(columns):
    taps = gauss_taps()
    wide = jnp.concatenate(columns + [jnp.zeros_like(columns[0])], axis=1)
    span = wide.shape[1]
    total = taps[RADIUS] * wide
    for i in range(1, RADIUS + 1):
        total = total + taps[RADIUS + i] * (pltpu.roll(wide, i, 1) + pltpu.roll(wide, span - i, 1))
    return total[:, : span - LANES]


def pair_weights(pair_epochs, days):
    pairs = pair_epochs.shape[1]
    first, second = pair_epochs[0:1], pair_epochs[1:2]
    step = iota((E, pairs), 0)
    design_t = jnp.where((first <= step) & (step < second), 1.0, 0.0)
    row, col = iota((LANES, pairs), 0), iota((LANES, pairs), 1)
    inside = (row < E) & (first <= row) & (row < second)
    other = jnp.where(inside | (row == col + E), 1.0, 0.0)
    system = lax.dot_general(
        design_t, other, (((1,), (1,)), ((), ())), precision=HIGHEST, preferred_element_type=jnp.float32
    )
    row, col = iota((E, LANES), 0), iota((E, LANES), 1)
    system = system + jnp.where((row == E - 1) & (col == E - 1), 1.0, 0.0)

    def eliminate(k, a):
        pivot_row = jnp.sum(jnp.where(row == k, a, 0.0), axis=0, keepdims=True)
        pivot_col = jnp.sum(jnp.where(col == k, a, 0.0), axis=1, keepdims=True)
        pivot = jnp.sum(jnp.where(row[:, 0:1] == k, pivot_col, 0.0), axis=0, keepdims=True)
        scaled = pivot_row / pivot
        return jnp.where(row == k, scaled, a - pivot_col * scaled)

    system = lax.fori_loop(0, E, eliminate, system)

    times = days.astype(jnp.float32)
    centred = (times - jnp.sum(times, axis=1, keepdims=True) / E) / 365.25
    phase = 2.0 * math.pi * times / 365.25
    erow, ecol = iota((E, E), 0), iota((E, E), 1)
    lane = ecol[0:1]
    eye = jnp.where(erow == ecol, 1.0, 0.0)
    q, q_t = eye, eye
    columns = [jnp.ones_like(times), centred, jnp.sin(phase), jnp.cos(phase)]
    for j in range(TERMS):
        below = jnp.where(lane >= j, columns[j], 0.0)
        head = jnp.sum(jnp.where(lane == j, below, 0.0), axis=1, keepdims=True)
        norm = jnp.sqrt(jnp.sum(below * below, axis=1, keepdims=True))
        v = below + jnp.where(lane == j, jnp.where(head >= 0, norm, -norm), 0.0)
        v = v * lax.rsqrt(0.5 * jnp.sum(v * v, axis=1, keepdims=True))
        upright = jnp.sum(jnp.where(erow == ecol, v, 0.0), axis=1, keepdims=True)
        columns = [c - v * jnp.sum(v * c, axis=1, keepdims=True) for c in columns]
        q = q - jnp.sum(q * v, axis=1, keepdims=True) * v
        q_t = q_t - upright * jnp.sum(q_t * upright, axis=0, keepdims=True)
    q = jnp.where(ecol >= TERMS, q, 0.0)
    q_t = jnp.where(erow >= TERMS, q_t, 0.0)
    summing = jnp.where(ecol < erow, 1.0, 0.0)
    displacement = jnp.dot(summing, system, precision=HIGHEST, preferred_element_type=jnp.float32)
    return q, jnp.dot(q_t, displacement, precision=HIGHEST, preferred_element_type=jnp.float32)


def spread_weights(weights, first, count):
    tall, wide, depth = E * STRIP, count * STRIP, weights.shape[1]
    right = jnp.where(iota((depth, wide), 0) == iota((depth, wide), 1) // STRIP + first, 1.0, 0.0)
    left = jnp.where(iota((tall, E), 1) == iota((tall, E), 0) // STRIP, 1.0, 0.0)
    full = jnp.dot(weights, right, precision=HIGHEST, preferred_element_type=jnp.float32)
    full = jnp.dot(left, full, precision=HIGHEST, preferred_element_type=jnp.float32)
    same = iota((tall, wide), 0) % STRIP == iota((tall, wide), 1) % STRIP
    return jnp.where(same, full, 0.0)


def times_stack(weights, stack):
    flat = stack.reshape(weights.shape[1], stack.shape[-1])
    total = jnp.dot(weights, flat, precision=HIGHEST, preferred_element_type=jnp.float32)
    return total.reshape(E, STRIP, stack.shape[-1])


def raw_strips(n_outer, strips):
    return 1 if n_outer > 1 and n_outer // 2 <= 2 else strips


def kernel(
    n_pair, n_quad, n_inner,
    x_hbm, small_hbm, out_hbm,
    padded, ready, held, gathered, summed, arrived, spread, result, small_ref,
    in_sem, small_sem, send_sem, recv_sem, gather_sem, sum_send_sem, sum_recv_sem, out_sem,
):
    local, height, width = ready.shape
    n = n_pair * n_quad
    n_outer = n_pair // n_inner
    half_n, half_pair = n // 2, n_pair // 2
    far = n_outer // 2
    rows, cols = height // n_pair, width // n_quad
    strips = rows // STRIP
    raw = raw_strips(n_outer, strips)
    tiles = width // LANES
    slab = lax.axis_index("slab")
    my_pair = lax.axis_index("pair")
    my_quad = lax.axis_index("quad")
    me = my_pair * n_quad + my_quad
    side = my_pair // half_pair
    my_source = me % half_n
    my_inner = my_pair % n_inner
    edge_outer = far - 1 + side

    loads = [
        pltpu.make_async_copy(
            x_hbm.at[l, :, pl.ds(j * LANES, LANES)],
            padded.at[l, j, pl.ds(STRIP, height), :],
            in_sem.at[l, j],
        )
        for l in range(local)
        for j in range(tiles)
    ]
    loads += [
        pltpu.make_async_copy(small_hbm, small_ref, small_sem.at[0]),
    ]
    for load in loads:
        load.start()
    barrier = pltpu.get_barrier_semaphore()

    def greet(j, carry):
        other = lax.rem(me + j, n)
        pl.semaphore_signal(
            barrier, inc=1, device_id=(slab, other // n_quad, other % n_quad), device_id_type=MESH
        )
        return carry

    lax.fori_loop(1, n, greet, 0)
    edge = jnp.zeros((local, tiles, STRIP, LANES), jnp.float32)
    padded[:, :, 0:STRIP, :] = edge
    padded[:, :, STRIP + height : 2 * STRIP + height, :] = edge
    if raw < strips:
        arrived[0:TERMS] = jnp.zeros((TERMS, rows, cols), jnp.float32)
    for load in loads:
        load.wait()
    pl.semaphore_wait(barrier, n - 1)

    def strip_rows(t):
        return pl.ds(pl.multiple_of(t * STRIP, STRIP), STRIP)

    def part(t, pair, quad):
        at_row = pl.multiple_of(pair * rows + t * STRIP, STRIP)
        at_col = pl.multiple_of(quad * cols, LANES)
        return ready.at[:, pl.ds(at_row, STRIP), pl.ds(at_col, cols)]

    def slot(t, source):
        return held.at[source, :, strip_rows(t), :]

    def gather_slot(t, at, source):
        return gathered.at[at, source, :, strip_rows(t), :]

    def send(t, pair, quad):
        return pltpu.make_async_remote_copy(
            src_ref=part(t, pair, quad),
            dst_ref=slot(t, me),
            send_sem=send_sem.at[t, pair * n_quad + quad],
            recv_sem=recv_sem.at[t, me],
            device_id=(slab, pair, quad),
            device_id_type=MESH,
        )

    def place(pair):
        return pair // n_inner - (1 - side) * far, edge_outer * n_inner + pair % n_inner

    def send_to_sum(t, pair, quad):
        at, target = place(pair)
        return pltpu.make_async_remote_copy(
            src_ref=part(t, pair, quad),
            dst_ref=gather_slot(t, at, my_source),
            send_sem=send_sem.at[t, pair * n_quad + quad],
            recv_sem=gather_sem.at[t, at, my_source],
            device_id=(slab, target, quad),
            device_id_type=MESH,
        )

    def smooth(t, pair):
        at_row = pl.multiple_of(pair * rows + t * STRIP, STRIP)
        for l in range(local):
            columns = [smooth_rows(padded.at[l, j], at_row) for j in range(tiles)]
            ready[l, pl.ds(at_row, STRIP), :] = smooth_columns(columns)

    def across(s):
        outer, inner = s // n_inner, (s + my_inner) % n_inner
        return ((1 - side) * (2 * far - 1 - outer) + side * outer) * n_inner + inner

    def produce_raw(i, carry):
        t, pair = i // half_pair, across(i % half_pair)
        smooth(t, pair)
        for j in range(n_quad):
            send(t, pair, (my_quad + j) % n_quad).start()
        return carry

    def produce_summed(i, carry):
        t, pair = raw + i // half_pair, across(i % half_pair)
        smooth(t, pair)
        at, target = place(pair)
        for j in range(1, n_quad):
            send_to_sum(t, pair, (my_quad + j) % n_quad).start()

        @pl.when(target != my_pair)
        def _():
            send_to_sum(t, pair, my_quad).start()

        @pl.when(target == my_pair)
        def _():
            pltpu.make_async_copy(
                part(t, pair, my_quad), gather_slot(t, at, my_source), gather_sem.at[t, at, my_source]
            ).start()

        return carry

    def produce_near(i, carry):
        t, s = i // half_pair, i % half_pair
        pair = side * half_pair + (my_pair + 1 + s) % half_pair
        smooth(t, pair)
        for j in range(1, n_quad):
            send(t, pair, (my_quad + j) % n_quad).start()

        @pl.when(pair != my_pair)
        def _():
            send(t, pair, my_quad).start()

        @pl.when(pair == my_pair)
        def _():
            pltpu.make_async_copy(part(t, my_pair, my_quad), slot(t, me), recv_sem.at[t, me]).start()

        return carry

    def sum_copy(t, at):
        return pltpu.make_async_remote_copy(
            src_ref=summed.at[at, pl.ds(TERMS, E - TERMS), strip_rows(t), :],
            dst_ref=arrived.at[pl.ds(TERMS, E - TERMS), strip_rows(t), :],
            send_sem=sum_send_sem.at[t, at],
            recv_sem=sum_recv_sem.at[t],
            device_id=(slab, ((1 - side) * far + at) * n_inner + my_inner, my_quad),
            device_id_type=MESH,
        )

    def add_up(i, carry):
        t, k = i // far, i % far
        at = (far - 1 - k) * (1 - side) + k * side

        def wait(source, carry):
            pltpu.make_async_copy(
                gather_slot(t, at, source), gather_slot(t, at, source), gather_sem.at[t, at, source]
            ).wait()
            return carry

        lax.fori_loop(0, half_n, wait, 0)
        summed[at, :, strip_rows(t), :] = times_stack(spread[2], gathered[at, :, :, strip_rows(t), :])
        sum_copy(t, at).start()
        return carry

    split = min(raw + 1, strips)
    lax.fori_loop(0, raw * half_pair, produce_raw, 0)
    lax.fori_loop(0, (split - raw) * half_pair, produce_summed, 0)

    q, v = pair_weights(small_ref[0:2], small_ref[2:3][:, :E])
    m = jnp.dot(q, v, precision=HIGHEST, preferred_element_type=jnp.float32)
    count = half_n * local
    spread[0] = spread_weights(m, E + side * count, count)
    spread[1] = spread_weights(m, E + (1 - side) * count, count)
    if raw < strips:
        spread[2] = spread_weights(v, E + side * count, count)
        spread[3] = spread_weights(q, 0, E)

    lax.fori_loop((split - raw) * half_pair, (strips - raw) * half_pair, produce_summed, 0)
    early = strips // 2 if raw < strips else strips
    lax.fori_loop(0, early * half_pair, produce_near, 0)

    if raw < strips:

        @pl.when(my_pair // n_inner == edge_outer)
        def _():
            lax.fori_loop(raw * far, split * far, add_up, 0)

        lax.fori_loop(early * half_pair, strips * half_pair, produce_near, 0)

        @pl.when(my_pair // n_inner == edge_outer)
        def _():
            lax.fori_loop(split * far, strips * far, add_up, 0)

    def wait_for(t, first):
        def wait(source, carry):
            pltpu.make_async_copy(slot(t, source), slot(t, source), recv_sem.at[t, source]).wait()
            return carry

        lax.fori_loop(first, first + half_n, wait, 0)

    def out_copy(t):
        return pltpu.make_async_copy(result.at[:, strip_rows(t), :], out_hbm.at[:, strip_rows(t), :], out_sem.at[t])

    def own_side(t, carry):
        wait_for(t, side * half_n)
        stack = held[pl.ds(side * half_n, half_n), :, strip_rows(t), :]
        result[:, strip_rows(t), :] = times_stack(spread[0], stack)
        return carry

    def far_side(t, carry):
        wait_for(t, (1 - side) * half_n)
        stack = held[pl.ds((1 - side) * half_n, half_n), :, strip_rows(t), :]
        result[:, strip_rows(t), :] += times_stack(spread[1], stack)
        out_copy(t).start()
        return carry

    def far_sums(t, carry):
        strip = arrived.at[pl.ds(TERMS, E - TERMS), strip_rows(t), :]
        pltpu.make_async_copy(strip, strip, sum_recv_sem.at[t]).wait()
        result[:, strip_rows(t), :] += times_stack(spread[3], arrived[:, strip_rows(t), :])
        out_copy(t).start()
        return carry

    lax.fori_loop(0, strips, own_side, 0)
    lax.fori_loop(0, raw, far_side, 0)
    if raw < strips:
        lax.fori_loop(raw, strips, far_sums, 0)

    def sent_raw(i, carry):
        t, other = i // half_n, (1 - side) * half_n + i % half_n
        send(t, other // n_quad, other % n_quad).wait_send()
        return carry

    def sent_summed(i, carry):
        t, other = raw + i // half_n, (1 - side) * half_n + i % half_n
        pair, quad = other // n_quad, other % n_quad

        @pl.when(place(pair)[1] * n_quad + quad != me)
        def _():
            send_to_sum(t, pair, quad).wait_send()

        return carry

    def sent_near(i, carry):
        t, other = i // (half_n - 1), side * half_n + (me + 1 + i % (half_n - 1)) % half_n
        send(t, other // n_quad, other % n_quad).wait_send()
        return carry

    def sent_sums(i, carry):
        sum_copy(i // far, i % far).wait_send()
        return carry

    lax.fori_loop(0, raw * half_n, sent_raw, 0)
    lax.fori_loop(0, strips * (half_n - 1), sent_near, 0)
    if raw < strips:
        lax.fori_loop(0, (strips - raw) * half_n, sent_summed, 0)

        @pl.when(my_pair // n_inner == edge_outer)
        def _():
            lax.fori_loop(raw * far, strips * far, sent_sums, 0)

    for t in range(strips):
        out_copy(t).wait()


def shards(n_inner, interferograms, pair_epochs, days):
    n_pair = lax.axis_size("pair")
    n_quad = lax.axis_size("quad")
    n = n_pair * n_quad
    local, height, width = interferograms.shape
    rows, cols = height // n_pair, width // n_quad
    strips = rows // STRIP
    far = n_pair // n_inner // 2
    sums = raw_strips(n_pair // n_inner, strips) < strips
    gathered = (far, n // 2, local, rows, cols) if sums else (1, 1, local, STRIP, LANES)
    summed = (far, E, rows, cols) if sums else (1, E, STRIP, LANES)
    short = pair_epochs.shape[1] - days.shape[0]
    small = jnp.concatenate([pair_epochs, jnp.pad(days, (0, short))[None, :]], axis=0)
    return pl.pallas_call(
        functools.partial(kernel, n_pair, n_quad, n_inner),
        out_shape=jax.ShapeDtypeStruct((E, rows, cols), jnp.float32),
        in_specs=[pl.BlockSpec(memory_space=pl.ANY)] * 2,
        out_specs=pl.BlockSpec(memory_space=pl.ANY),
        scratch_shapes=[
            pltpu.VMEM((local, width // LANES, height + 2 * STRIP, LANES), jnp.float32),
            pltpu.VMEM((local, height, width), jnp.float32),
            pltpu.VMEM((n, local, rows, cols), jnp.float32),
            pltpu.VMEM(gathered, jnp.float32),
            pltpu.VMEM(summed, jnp.float32),
            pltpu.VMEM(summed[1:], jnp.float32),
            pltpu.VMEM((4, E * STRIP, n // 2 * local * STRIP), jnp.float32),
            pltpu.VMEM((E, rows, cols), jnp.float32),
            pltpu.VMEM(small.shape, jnp.int32),
            pltpu.SemaphoreType.DMA((local, width // LANES)),
            pltpu.SemaphoreType.DMA((1,)),
            pltpu.SemaphoreType.DMA((strips, n)),
            pltpu.SemaphoreType.DMA((strips, n)),
            pltpu.SemaphoreType.DMA((strips, far, n // 2) if sums else (1, 1, 1)),
            pltpu.SemaphoreType.DMA((strips, far)),
            pltpu.SemaphoreType.DMA((strips,)),
            pltpu.SemaphoreType.DMA((strips,)),
        ],
        compiler_params=pltpu.CompilerParams(
            collective_id=0, has_side_effects=True, vmem_limit_bytes=48 * 1024 * 1024
        ),
        name="smooth_and_invert",
    )(interferograms, small)


def inner_size(mesh):
    line = list(mesh.devices[0, :, 0])
    coords = [getattr(d, "coords", None) for d in line]
    if any(c is None for c in coords):
        return 1
    moving = [k for k in range(len(coords[0])) if coords[0][k] != coords[-1][k]]
    for k in moving:
        run = 1
        while run < len(line) and coords[run][k] == coords[0][k]:
            run += 1
        if 1 < run < len(line) and len(line) % run == 0:
            return run
    return 1


def solution(mesh):
    placed = (P(("pair", "quad"), "slab", None), P(), P())
    return jax.shard_map(
        functools.partial(shards, inner_size(mesh)),
        mesh=mesh,
        in_specs=placed,
        out_specs=P(None, ("slab", "pair"), "quad"),
        check_vma=False,
    )
```
